512 devices in a mesh: row: 32 (over z, x), col: 16 (over y, core).
Axes of the slice: x: 4, y: 8, z: 8, core: 2. Of those that a mesh axis runs over, the one named last changes fastest.
Arguments:
- tiles: float32 [8192, 128, 128], P(('row', 'col')), may hold values from -1 to 1
- coords: int32 [8192, 2], P(('row', 'col')), may hold values from 0 to 4095, as said below
- counts: int32 [512], P(('row', 'col')), may hold values from 8 to 16
- probes: bfloat16 [64, 16, 32768], P(None, 'col', 'row'), may hold values from -6 to 6
Outputs:
- q_basis: float32 [64, 131072], P(None, ('row', 'col'))
- w_basis: bfloat16 [64, 16, 32768], P(None, 'col', 'row')
- r_factor: float32 [64, 64], replicated
The draws below stay inside these ranges and needn't reach their ends.
Inputs may be any that keep to these rules, and one draw needn't show every extreme that they name: `coords`: slots are ordered by device, row index first, 16 slots a device. The slots of device (r, c) name block rows r * 32 to (r + 1) * 32 - 1 and block columns c * 256 to (c + 1) * 256 - 1. Shares are the aligned runs of 8 block columns. Among the live slots of one device at most 1 name block columns of one share. Pairs may repeat; their tiles then add.
All inputs are finite; a program needn't handle non-finite values.
Results may differ from the reference program's by a relative error of at most 0.0012.
Values may be sent and summed in bfloat16 or wider, within the bound.
A program may use at most 64 MiB of HBM per device.

```python
import jax
import jax.numpy as jnp
from jax import lax

P_SIZE = 64
BLOCK = 128
NCOLS = 524288
RB_DEV = 32
CAP = 16
ROWS = 131072
COLS_GROUP = 32768
CBR = 8
CBG = 256
SLOTS = 1
N_ROW = 32
N_COL = 16
DEVICES = 512


def tile_layout(key):
    devices = N_ROW * N_COL
    hot_col = jax.random.randint(jax.random.fold_in(key, 101), (N_COL,), 0, N_ROW)
    hot_col = hot_col.at[0].set(0)
    hot_col = hot_col.at[N_COL - 1].set(N_ROW - 1)
    hot_dev = hot_col[jnp.arange(devices) % N_COL]
    seat_keys = jax.random.split(jax.random.fold_in(key, 102), devices)

    def shuffle_seats(seat_key):
        return jax.random.permutation(seat_key, (N_ROW - 1) * SLOTS)[:CAP - SLOTS]
    seats = jax.vmap(shuffle_seats)(seat_keys)
    others = seats // SLOTS
    others = others + (others >= hot_dev[:, None]).astype(jnp.int32)
    owners = jnp.concatenate([jnp.repeat(hot_dev[:, None], SLOTS, axis=1), others], axis=1).reshape(-1)
    device = jnp.arange(CAP * devices) // CAP
    within = jax.random.randint(jax.random.fold_in(key, 103), (CAP * devices,), 0, CBR)
    offset = jax.random.randint(jax.random.fold_in(key, 104), (CAP * devices,), 0, RB_DEV)
    last_slot = (devices - 1) * CAP
    within = within.at[0].set(0).at[last_slot].set(CBR - 1)
    offset = offset.at[0].set(0).at[last_slot].set(RB_DEV - 1)
    rows = device // N_COL * RB_DEV + offset
    cols = device % N_COL * CBG + owners * CBR + within
    return (rows.astype(jnp.int32), cols.astype(jnp.int32))


def draw_coords(key, part):
    rows, cols = tile_layout(key)
    return jnp.stack([rows, cols], axis=1)


def draw_tiles(key, part):
    rows, cols = tile_layout(key)
    key = jax.random.fold_in(key, 5)
    first, second, third = jax.random.split(key, 3)
    entries = jax.random.normal(third, (CAP * N_ROW * N_COL, BLOCK, BLOCK), jnp.float32)
    power = 1.0
    low_end = 0.5
    high_end = 5.0
    row_table = jnp.exp(jax.random.uniform(first, (ROWS,), jnp.float32, jnp.log(low_end), jnp.log(high_end)))
    col_table = jnp.exp(jax.random.uniform(second, (NCOLS,), jnp.float32, jnp.log(low_end), jnp.log(high_end)))
    lane = jnp.arange(BLOCK)
    row_index = rows[:, None] * BLOCK + lane[None, :]
    col_index = cols[:, None] * BLOCK + lane[None, :]
    col_inside = (cols % CBG)[:, None] * BLOCK + lane[None, :]
    row_rise = (1.0 + 2.0 * row_index.astype(jnp.float32) / ROWS) ** power
    col_rise = (1.0 + 2.0 * col_inside.astype(jnp.float32) / COLS_GROUP) ** power
    row_factor = row_rise * row_table[row_index]
    col_factor = col_rise * col_table[col_index]
    base = 0.25 * (4.0 * RB_DEV / (3.0 * N_COL * CAP * BLOCK)) ** 0.5
    values = entries * base * row_factor[:, :, None] * col_factor[:, None, :]
    return jnp.clip(values, -1.0, 1.0)


def draw_counts(key, part):
    key = jax.random.fold_in(key, 9)
    first, second = jax.random.split(key)
    number = jax.random.randint(first, (DEVICES,), CAP // 2, CAP + 1)
    picked = jax.random.permutation(second, DEVICES)[:2]
    number = number.at[picked[0]].set(CAP)
    number = number.at[picked[1]].set(CAP // 2)
    return number.astype(jnp.int32)


def shard_levels(own_key, dims, shards, smallest, high):
    def one(position, blocks):
        heights = jax.random.uniform(jax.random.fold_in(jax.random.fold_in(own_key, 6), position), (blocks,), jnp.float32, smallest / len(shards), high / len(shards))
        return jnp.repeat(jnp.exp(heights), dims[position] // blocks).reshape((-1,) + (1,) * (len(dims) - position - 1))

    gain = one(*shards[0])
    for cut in shards[1:]:
        gain = gain * one(*cut)
    return gain


def centred(key, extent, scale, limit, shards=(), kind=jnp.bfloat16):
    values = scale * jax.random.normal(key, extent, jnp.float32)
    if shards:
        values = values * shard_levels(key, extent, shards, -0.22, 0.18)
    return jnp.clip(values, -limit, limit).astype(kind)


def setup_inputs(seed: int = 0) -> dict:
    arg_keys = jax.random.split(jax.random.key(seed), 5)
    tiles = draw_tiles(jax.random.fold_in(arg_keys[4], 71), 0)
    coords = draw_coords(jax.random.fold_in(arg_keys[4], 71), 0)
    counts = draw_counts(jax.random.fold_in(arg_keys[4], 71), 0)
    probes = centred(arg_keys[3], (P_SIZE, N_COL, COLS_GROUP), 1.0, 6.0, ((1, 16), (2, 32)))
    return {"tiles": tiles, "coords": coords, "counts": counts, "probes": probes}


highest = lax.Precision.HIGHEST

def lower_inverse(lower):
    size = lower.shape[0]
    ident = jnp.eye(size, dtype=jnp.float32)

    def advance(index, result):
        line = lower[index]
        value = (ident[index] - jnp.dot(line, result, precision=highest)) / line[index]
        return result.at[index].set(value)
    return lax.fori_loop(0, size, advance, jnp.zeros_like(lower))

def orthonormal(matrix, count):
    gram = jnp.dot(matrix.astype(jnp.float32), matrix.T.astype(jnp.float32), preferred_element_type=jnp.float32, precision=highest)
    lower = jnp.linalg.cholesky(gram / count)
    result = jnp.dot(lower_inverse(lower).astype(jnp.float32), matrix.astype(jnp.float32), preferred_element_type=jnp.float32, precision=highest)
    return (result, lower)

def sketch_rows(strip, tiles4, rows4, cols4, mask4):

    def step(total, item):
        tile, rows, cols, keep = item
        blocks = jnp.take(strip, cols, axis=1).astype(jnp.float32)
        contrib = jnp.einsum('ptk,tik->pti', blocks, tile, precision=highest) * keep[None, :, None]
        return (total.at[:, rows, :].add(contrib), None)
    start = jnp.zeros((P_SIZE, ROWS // BLOCK, BLOCK), jnp.float32)
    total, unused = lax.scan(step, start, (tiles4, rows4, cols4, mask4))
    return total.reshape(P_SIZE, ROWS)

def sketch_cols(basis, tiles4, rows4, cols4, mask4):
    source = basis.reshape(P_SIZE, ROWS // BLOCK, BLOCK)

    def step(total, item):
        tile, rows, cols, keep = item
        blocks = jnp.take(source, rows, axis=1)
        contrib = jnp.einsum('pti,tik->ptk', blocks, tile, precision=highest) * keep[None, :, None]
        return (total.at[:, cols, :].add(contrib), None)
    start = jnp.zeros((P_SIZE, NCOLS // BLOCK, BLOCK), jnp.float32)
    total, unused = lax.scan(step, start, (tiles4, rows4, cols4, mask4))
    return total.reshape(P_SIZE, NCOLS)

def reference(tiles, coords, counts, probes):
    slot = jnp.arange(CAP * DEVICES, dtype=jnp.int32)
    keep = (slot % CAP < jnp.repeat(counts, CAP)).astype(jnp.float32)
    tiles4 = tiles.reshape(DEVICES, CAP, BLOCK, BLOCK)
    rows4 = coords[:, 0].reshape(DEVICES, CAP)
    cols4 = coords[:, 1].reshape(DEVICES, CAP)
    mask4 = keep.reshape(DEVICES, CAP)
    strip = probes.reshape(P_SIZE, NCOLS // BLOCK, BLOCK)
    sketch_one = sketch_rows(strip, tiles4, rows4, cols4, mask4)
    basis_one, lower_one = orthonormal(sketch_one, ROWS)
    columns = sketch_cols(basis_one, tiles4, rows4, cols4, mask4)
    spread, lower_cols = orthonormal(columns, NCOLS)
    w_basis = spread.astype(jnp.bfloat16)
    sketch_two = sketch_rows(w_basis.reshape(P_SIZE, NCOLS // BLOCK, BLOCK), tiles4, rows4, cols4, mask4)
    q_basis, lower_two = orthonormal(sketch_two, ROWS)
    return (q_basis, w_basis.reshape(P_SIZE, N_COL, COLS_GROUP), lower_two.T)
```

```python
import functools

import jax
import jax.numpy as jnp
from jax import lax
from jax.experimental import pallas as pl
from jax.experimental.pallas import tpu as pltpu
from jax.sharding import PartitionSpec as P

MESH = pl.DeviceIdType.MESH
highest = lax.Precision.HIGHEST
f32 = jnp.float32
bf16 = jnp.bfloat16
LANE = 128
CORES = 2
CHUNKS = 2


def nn(left, right):
    return lax.dot_general(
        left, right, (((1,), (0,)), ((), ())), precision=highest, preferred_element_type=f32
    )


def nt(left, right):
    return lax.dot_general(
        left, right, (((1,), (1,)), ((), ())), precision=highest, preferred_element_type=f32
    )


def remote(src, dst, send, recv, device):
    return pltpu.make_async_remote_copy(
        src_ref=src,
        dst_ref=dst,
        send_sem=send,
        recv_sem=recv,
        device_id=device,
        device_id_type=MESH,
    )


def loop(lower, upper, body):
    def step(i, carry):
        body(i)
        return carry

    lax.fori_loop(lower, upper, step, 0)


def offset(k, n):
    step = (k + 1) // 2
    return n // 2 + step * (2 * lax.rem(k, 2) - 1)


def greet(n_row, n_col, row, col, with_row, with_col):
    barrier = pltpu.get_barrier_semaphore()
    count = 0
    if with_row:
        loop(
            1,
            n_row,
            lambda d: pl.semaphore_signal(
                barrier, inc=1, device_id=(lax.rem(row + d, n_row), col), device_id_type=MESH
            ),
        )
        count += n_row - 1
    if with_col:
        loop(
            1,
            n_col,
            lambda d: pl.semaphore_signal(
                barrier, inc=1, device_id=(row, lax.rem(col + d, n_col)), device_id_type=MESH
            ),
        )
        count += n_col - 1
    pl.semaphore_wait(barrier, count)


class Exchange:
    def __init__(self, n, me, source, dst, send, recv, device):
        self.n, self.me, self.source, self.dst = n, me, source, dst
        self.send, self.recv, self.device = send, recv, device

    def copy_to(self, peer):
        return remote(
            self.source(peer),
            self.dst.at[self.me],
            self.send.at[peer],
            self.recv.at[self.me],
            self.device(peer),
        )

    def copy_from(self, peer):
        return remote(
            self.source(peer),
            self.dst.at[peer],
            self.send.at[peer],
            self.recv.at[peer],
            self.device(peer),
        )

    def start(self):
        loop(
            0, self.n - 1, lambda k: self.copy_to(lax.rem(self.me + offset(k, self.n), self.n)).start()
        )

    def wait(self):
        loop(
            0,
            self.n - 1,
            lambda k: self.copy_from(lax.rem(self.me - offset(k, self.n) + self.n, self.n)).wait(),
        )


def sum_slots(ref, n):
    total = ref[0]
    for s in range(1, n):
        total = total + ref[s]
    return total


def pack_gram(block):
    size = block.shape[0]
    half = size // 2
    zero = jnp.zeros_like(block)
    return nt(block[:half], jnp.concatenate([block, zero], axis=0)) + nt(
        block[half:], jnp.concatenate([zero, block], axis=0)
    )


class GramSum:
    def __init__(self, sizes, row, col, r, tag):
        n_row, n_col, nx = sizes
        nz = n_row // nx
        z, x = row // nx, lax.rem(row, nx)
        self.nx, self.nz, self.nc, self.x, self.z, self.col = nx, nz, n_col, x, z, col
        get = lambda name: r[tag + name]
        self.part, self.gx, self.s1, self.gz = get("part"), get("gx"), get("s1"), get("gz")
        self.s2, self.gc, self.out = get("s2"), get("gc"), get("out")
        along_x = lambda p: (z * nx + p, col)
        along_z = lambda p: (p * nx + x, col)
        along_c = lambda p: (row, p)
        part, s1, s2, out = self.part, self.s1, self.s2, self.out
        self.first = Exchange(
            nx, x, lambda p: part.at[p], self.gx, get("x_send"), get("x_recv"), along_x
        )
        self.second = Exchange(nz, z, lambda p: s1, self.gz, get("z_send"), get("z_recv"), along_z)
        self.third = Exchange(
            n_col, col, lambda p: s2, self.gc, get("c_send"), get("c_recv"), along_c
        )
        self.last = Exchange(
            nx, x, lambda p: out.at[x], out, get("o_send"), get("o_recv"), along_x
        )

    def scatter_x(self, packed):
        depth = packed.shape[0] // self.nx
        for j in range(self.nx):
            self.part[j] = packed[j * depth : (j + 1) * depth]
        self.first.start()
        self.gx[self.x] = self.part[self.x]

    def sum_z(self):
        self.first.wait()
        self.s1[...] = sum_slots(self.gx, self.nx)
        self.second.start()
        self.gz[self.z] = self.s1[...]

    def sum_columns(self):
        self.second.wait()
        self.s2[...] = sum_slots(self.gz, self.nz)
        self.third.start()
        self.gc[self.col] = self.s2[...]

    def gather_x(self):
        self.third.wait()
        self.out[self.x] = sum_slots(self.gc, self.nc)
        self.last.start()

    def result(self):
        self.last.wait()
        return self.out[...].reshape(32, LANE)


def gram_scratch(sizes, tag):
    n_row, n_col, nx = sizes
    depth = 32 // nx
    nz = n_row // nx
    dma = pltpu.SemaphoreType.DMA
    named = {
        "part": pltpu.VMEM((nx, depth, LANE), f32),
        "gx": pltpu.VMEM((nx, depth, LANE), f32),
        "s1": pltpu.VMEM((depth, LANE), f32),
        "gz": pltpu.VMEM((nz, depth, LANE), f32),
        "s2": pltpu.VMEM((depth, LANE), f32),
        "gc": pltpu.VMEM((n_col, depth, LANE), f32),
        "out": pltpu.VMEM((nx, depth, LANE), f32),
        "x_send": dma((nx,)),
        "x_recv": dma((nx,)),
        "z_send": dma((nz,)),
        "z_recv": dma((nz,)),
        "c_send": dma((n_col,)),
        "c_recv": dma((n_col,)),
        "o_send": dma((nx,)),
        "o_recv": dma((nx,)),
    }
    return {tag + name: shape for name, shape in named.items()}


def pick(own, wanted):
    wanted = jnp.broadcast_to(wanted, (own.shape[0], LANE))
    total = jnp.zeros((own.shape[0], LANE), f32)
    for b in range(own.shape[1] // LANE):
        total = jnp.where(wanted == b + 1, own[:, b * LANE : (b + 1) * LANE].astype(f32), total)
    return total.astype(bf16)


class Spread:
    def __init__(self, n_row, row, col, chunks, r, tag):
        self.n_row, self.row, self.chunks = n_row, row, chunks
        self.wanted = r["wanted"]
        self.outgoing = [r[tag + "outgoing%d" % c] for c in range(chunks)]
        self.got = [r[tag + "got%d" % c] for c in range(chunks)]
        self.moves = [
            Exchange(
                n_row,
                row,
                functools.partial(lambda ref, p: ref.at[p], self.outgoing[c]),
                self.got[c],
                r[tag + "send%d" % c],
                r[tag + "recv%d" % c],
                lambda p: (p, col),
            )
            for c in range(chunks)
        ]

    def store(self, refs, place, block):
        rows = block.shape[0] // self.chunks
        for c in range(self.chunks):
            refs[c][place] = block[c * rows : (c + 1) * rows]

    def start(self, own_ref, ready=None):
        def serve(k):
            peer = lax.rem(self.row - offset(k, self.n_row) + self.n_row, self.n_row)
            if ready is not None:
                ready(peer)
            self.store(self.outgoing, peer, pick(own_ref[...], self.wanted[peer]))
            self.moves[0].copy_to(peer).start()

        loop(0, self.n_row - 1, serve)
        self.store(self.got, self.row, pick(own_ref[...], self.wanted[self.row]))

    def finish(self, c):
        def step(k):
            peer = lax.rem(self.row - offset(k, self.n_row) + self.n_row, self.n_row)
            self.moves[c].copy_from(peer).wait()
            if c + 1 < self.chunks:
                self.moves[c + 1].copy_to(peer).start()

        loop(0, self.n_row - 1, step)


def spread_scratch(n_row, chunks, width, tag):
    rows = width // chunks
    named = {}
    for c in range(chunks):
        named[tag + "outgoing%d" % c] = pltpu.VMEM((n_row, rows, LANE), bf16)
        named[tag + "got%d" % c] = pltpu.VMEM((n_row, rows, LANE), bf16)
        named[tag + "send%d" % c] = pltpu.SemaphoreType.DMA((n_row,))
        named[tag + "recv%d" % c] = pltpu.SemaphoreType.DMA((n_row,))
    return named


class RowSums:
    def __init__(self, n_col, row, col, c, r, tag):
        self.ny = ny = n_col // CORES
        self.n_col = n_col
        self.y, self.core = col // CORES, lax.rem(col, CORES)
        self.row, self.col = row, col
        self.other = col + 1 - 2 * self.core
        get = lambda name: r[tag + name + "%d" % c]
        self.terms, self.part, self.near = get("contrib"), get("rows"), get("near")
        self.near_send, self.near_recv = get("near_send"), get("near_recv")
        self.summed, self.far = get("summed"), get("far")
        self.shares = Exchange(
            ny,
            self.y,
            lambda p: self.summed.at[p],
            self.far,
            get("far_send"),
            get("far_recv"),
            self.same_core,
        )
        if tag + "group%d" % c in r:
            self.group = get("group")
            self.all_send, self.all_recv = get("all_send"), get("all_recv")
            self.pass_send, self.pass_recv = get("pass_send"), get("pass_recv")

    def same_core(self, p):
        return (self.row, p * CORES + self.core)

    def near_copy(self, t):
        return remote(
            self.part.at[t * CORES + (1 - self.core)],
            self.near.at[t],
            self.near_send.at[t],
            self.near_recv.at[t],
            (self.row, self.other),
        )

    def peer(self, k):
        return lax.rem(self.y + offset(k, self.ny), self.ny)

    def sketch(self, got, splits, info):
        capacity = splits[0].shape[0]
        dims = (((1,), (1,)), ((), ()))
        for t in range(capacity):
            block = got[info["owner"](t)]
            total = lax.dot_general(block, splits[2][t], dims, preferred_element_type=f32)
            total += lax.dot_general(block, splits[1][t], dims, preferred_element_type=f32)
            total += lax.dot_general(block, splits[0][t], dims, preferred_element_type=f32)
            self.terms[t] = total
        self.terms[capacity] = jnp.zeros(self.terms.shape[1:], f32)

        def chain(t):
            self.terms[t] = self.terms[t] + self.terms[info["before"](t)]

        loop(0, capacity, chain)

        def place(p):
            for j in range(2):
                self.part[p, j] = self.terms[info["last"](2 * p + j)]

        loop(0, self.n_col, place)

    def start(self):
        loop(0, self.ny - 1, lambda k: self.near_copy(self.peer(k)).start())
        self.near_copy(self.y).start()

    def pair_up(self):
        def step(k):
            peer = self.peer(k)
            self.near_copy(peer).wait()
            self.summed[peer] = self.part[peer * CORES + self.core] + self.near[peer]
            self.shares.copy_to(peer).start()

        loop(0, self.ny - 1, step)
        self.near_copy(self.y).wait()
        self.far[self.y] = self.part[self.y * CORES + self.core] + self.near[self.y]

    def total(self):
        self.shares.wait()
        return sum_slots(self.far, self.ny)

    def pass_copy(self, slot, peer):
        return remote(
            self.group.at[slot],
            self.group.at[slot],
            self.pass_send.at[peer],
            self.pass_recv.at[peer],
            (self.row, self.other),
        )

    def gather(self, total):
        self.group[self.col] = total
        mine = self.group.at[self.col]

        def send(k):
            peer = self.peer(k)
            remote(
                mine, mine, self.all_send.at[peer], self.all_recv.at[self.y], self.same_core(peer)
            ).start()

        loop(0, self.ny - 1, send)
        self.pass_copy(self.col, self.y).start()

    def gathered(self):
        def relay(k):
            peer = lax.rem(self.y - offset(k, self.ny) + self.ny, self.ny)
            slot = peer * CORES + self.core
            remote(
                self.group.at[self.col],
                self.group.at[slot],
                self.all_send.at[peer],
                self.all_recv.at[peer],
                self.same_core(peer),
            ).wait()
            self.pass_copy(slot, peer).start()

        loop(0, self.ny - 1, relay)
        loop(0, self.ny, lambda p: self.pass_copy(p * CORES + (1 - self.core), p).wait())


def row_scratch(n_col, capacity, chunks, width, tag, gather):
    ny = n_col // CORES
    rows = width // chunks
    dma = pltpu.SemaphoreType.DMA
    named = {}
    for c in range(chunks):
        some = {
            "contrib": pltpu.VMEM((capacity + 1, rows, LANE), f32),
            "rows": pltpu.VMEM((n_col, 2, rows, LANE), f32),
            "near": pltpu.VMEM((ny, 2, rows, LANE), f32),
            "summed": pltpu.VMEM((ny, 2, rows, LANE), f32),
            "far": pltpu.VMEM((ny, 2, rows, LANE), f32),
        }
        sems = ["near_send", "near_recv", "far_send", "far_recv"]
        if gather:
            some["group"] = pltpu.VMEM((n_col, 2, rows, LANE), f32)
            sems += ["all_send", "all_recv", "pass_send", "pass_recv"]
        for name in sems:
            some[name] = dma((ny,))
        for name, shape in some.items():
            named[tag + name + "%d" % c] = shape
    return named


def three(value):
    high = value.astype(bf16)
    rest = value - high.astype(f32)
    middle = rest.astype(bf16)
    return high, middle, (rest - middle.astype(f32)).astype(bf16)


class ColumnSums:
    def __init__(self, n_row, row, col, c, r):
        self.n_row, self.row = n_row, row
        self.terms, self.outgoing, self.arrived = (
            r["terms%d" % c],
            r["leaving%d" % c],
            r["arrived%d" % c],
        )
        self.wanted = r["wanted"]
        self.moved = Exchange(
            n_row,
            row,
            lambda p: self.outgoing.at[p],
            self.arrived,
            r["leaving_send%d" % c],
            r["leaving_recv%d" % c],
            lambda p: (p, col),
        )

    def start(self, group, splits, info):
        capacity = splits[0].shape[0]
        rows = self.terms.shape[1]

        def dot(left, right):
            return lax.dot_general(
                left, right, (((1,), (0,)), ((), ())), preferred_element_type=f32
            )

        for t in range(capacity):
            place = info["place"](t)
            source = group[place // 2, lax.rem(place, 2)]
            high, middle, low = three(source)
            by_high = dot(jnp.concatenate([high, middle, low], axis=0), splits[0][t])
            by_middle = dot(jnp.concatenate([high, middle], axis=0), splits[1][t])
            by_low = dot(high, splits[2][t])
            small = by_high[2 * rows :] + by_middle[rows:] + by_low
            self.terms[t] = by_high[:rows] + (by_high[rows : 2 * rows] + by_middle[:rows] + small)
        self.terms[capacity] = jnp.zeros(self.terms.shape[1:], f32)

        def serve(k):
            peer = lax.rem(self.row + offset(k, self.n_row), self.n_row)
            self.outgoing[peer] = self.terms[info["slot"](peer)]
            self.moved.copy_to(peer).start()

        loop(0, self.n_row - 1, serve)
        self.arrived[self.row] = self.terms[info["slot"](self.row)]

    def finish(self, columns_ref, first):
        self.moved.wait()
        rows = self.arrived.shape[1]

        def column(b):
            def add(s, total):
                hit = jnp.broadcast_to(self.wanted[s], (rows, LANE)) == b + 1
                return total + jnp.where(hit, self.arrived[s], 0.0)

            columns_ref[b, first : first + rows] = lax.fori_loop(
                0, self.n_row, add, jnp.zeros((rows, LANE), f32)
            )

        loop(0, columns_ref.shape[0], column)


def column_scratch(n_row, capacity, chunks, width):
    rows = width // chunks
    named = {}
    for c in range(chunks):
        named["terms%d" % c] = pltpu.VMEM((capacity + 1, rows, LANE), f32)
        named["leaving%d" % c] = pltpu.VMEM((n_row, rows, LANE), f32)
        named["arrived%d" % c] = pltpu.VMEM((n_row, rows, LANE), f32)
        named["leaving_send%d" % c] = pltpu.SemaphoreType.DMA((n_row,))
        named["leaving_recv%d" % c] = pltpu.SemaphoreType.DMA((n_row,))
    return named


def loop_factor(packed, count, work):
    lane = lax.broadcasted_iota(jnp.int32, (64, LANE), 1)
    line = lax.broadcasted_iota(jnp.int32, (64, LANE), 0)
    sub = lax.broadcasted_iota(jnp.int32, (8, LANE), 0)
    gram = jnp.concatenate([packed, pltpu.roll(packed, 64, 1)], axis=0) * (1.0 / count)
    work[...] = jnp.where(lane < 64, gram, jnp.where(lane - 64 == line, 1.0, 0.0))

    def eliminate(kb):
        base = pl.multiple_of(kb * 8, 8)
        shift = lax.rem(LANE - base, LANE)
        block = work[pl.ds(base, 8), :]
        whole = work[...]
        near = pltpu.roll(block, shift, 1)
        far = pltpu.roll(whole, shift, 1)
        heads = [jnp.broadcast_to(near[:, i : i + 1], (8, LANE)) for i in range(8)]
        cols = [jnp.broadcast_to(far[:, i : i + 1], (64, LANE)) for i in range(8)]
        lines = [jnp.broadcast_to(block[i : i + 1, :], (8, LANE)) for i in range(8)]
        diagonal = jnp.ones((8, LANE), f32)
        total = jnp.zeros((64, LANE), f32)
        final = lines[0]
        for i in range(8):
            pivot = jnp.broadcast_to(heads[i][i : i + 1, :], (8, LANE))
            diagonal = jnp.where(sub == i, pivot, diagonal)
            final = jnp.where(sub == i, lines[i], final)
            inverse = 1.0 / pivot
            scaled = lines[i] * inverse
            total = total + cols[i] * jnp.broadcast_to(scaled[:1], (64, LANE))
            for j in range(i + 1, 8):
                ratio = jnp.broadcast_to(heads[i][j : j + 1, :], (8, LANE)) * inverse
                lines[j] = lines[j] - ratio * lines[i]
                heads[j] = heads[j] - heads[i] * ratio
                cols[j] = cols[j] - cols[i] * jnp.broadcast_to(ratio[:1], (64, LANE))
        work[...] = whole - jnp.where(line >= base + 8, total, 0.0)
        work[pl.ds(base, 8), :] = final / jnp.sqrt(diagonal)

    loop(0, 8, eliminate)


def inverse_of(work):
    both = work[...]
    lane = lax.broadcasted_iota(jnp.int32, both.shape, 1)
    return jnp.where(lane < 64, pltpu.roll(both, 64, 1), 0.0)


def whole_kernel(sizes, chunks, totals, names, info_ref, tiles_ref, own_ref, ids_ref, *refs):
    n_row, n_col, nx = sizes
    total_rows, total_cols = totals
    held_ref, gram_ref, basis_ref = refs[:3]
    r = dict(zip(names, refs[3:]))
    row, col = lax.axis_index("row"), lax.axis_index("col")
    capacity = tiles_ref.shape[0]
    starts = {"owner": 0, "place": capacity, "before": 2 * capacity, "last": 3 * capacity}
    starts["slot"] = 3 * capacity + 2 * n_col
    info = {
        name: functools.partial(lambda first, i: info_ref[first + i], first)
        for name, first in starts.items()
    }
    splits = [r["high"], r["middle"], r["low"]]
    wanted = r["wanted"]
    width = own_ref.shape[0]
    rows = width // chunks
    columns_ref, work, held = r["columns"], r["work"], r["held"]

    greet(n_row, n_col, row, col, True, True)
    ids = Exchange(
        n_row,
        row,
        lambda p: ids_ref.at[p],
        wanted,
        r["id_send"],
        r["id_recv"],
        lambda p: (p, col),
    )
    ids.start()
    wanted[row] = ids_ref[row]

    def split(t):
        for ref, piece in zip(splits, three(tiles_ref[t])):
            ref[t] = piece

    loop(0, capacity, split)

    spread = Spread(n_row, row, col, chunks, r, "one_")
    sums = [RowSums(n_col, row, col, c, r, "one_") for c in range(chunks)]
    spread.start(own_ref, lambda peer: ids.copy_from(peer).wait())
    for c in range(chunks):
        spread.finish(c)
        sums[c].sketch(spread.got[c], splits, info)
        sums[c].start()
        sums[c].pair_up()
    for c in range(chunks):
        total = sums[c].total()
        sums[c].gather(total)
        held[:, c * rows : (c + 1) * rows] = total
    gram_one = GramSum(sizes, row, col, r, "gram_one_")
    gram_one.scatter_x(pack_gram(held[0]) + pack_gram(held[1]))
    moves = [ColumnSums(n_row, row, col, c, r) for c in range(chunks)]
    steps = [gram_one.sum_z, gram_one.sum_columns, gram_one.gather_x]
    for c in range(chunks):
        sums[c].gathered()
        if c + 1 == chunks:
            for step in steps[1:]:
                step()
        elif c == 0:
            steps[0]()
        moves[c].start(sums[c].group, splits, info)
    if chunks == 1:
        for step in steps:
            step()
    loop_factor(gram_one.result(), total_rows, work)
    inverse_one = inverse_of(work)
    for c in range(chunks):
        moves[c].finish(columns_ref, c * rows)

    def normalise(b, packed):
        block = apply_inverse(inverse_one, columns_ref[b])
        columns_ref[b] = block
        return packed + pack_gram(block)

    packed = lax.fori_loop(0, columns_ref.shape[0], normalise, jnp.zeros((32, LANE), f32))
    gram_cols = GramSum(sizes, row, col, r, "gram_cols_")
    gram_cols.scatter_x(packed)
    gram_cols.sum_z()
    gram_cols.sum_columns()
    gram_cols.gather_x()
    loop_factor(gram_cols.result(), total_cols, work)
    inverse_cols = inverse_of(work)
    for b in range(columns_ref.shape[0]):
        basis_ref[:, b * LANE : (b + 1) * LANE] = apply_inverse(inverse_cols, columns_ref[b]).astype(
            bf16
        )

    spread = Spread(n_row, row, col, chunks, r, "two_")
    sums = [RowSums(n_col, row, col, c, r, "two_") for c in range(chunks)]
    spread.start(basis_ref)
    for c in range(chunks):
        spread.finish(c)
        sums[c].sketch(spread.got[c], splits, info)
        sums[c].start()
        sums[c].pair_up()
    for c in range(chunks):
        held_ref[:, c * rows : (c + 1) * rows] = sums[c].total()
    gram_two = GramSum(sizes, row, col, r, "gram_two_")
    gram_two.scatter_x(pack_gram(held_ref[0]) + pack_gram(held_ref[1]))
    gram_two.sum_z()
    gram_two.sum_columns()
    gram_two.gather_x()
    gram_ref[...] = gram_two.result()


def whole_scratch(sizes, chunks, capacity, width, per_owner, block):
    n_row, n_col, nx = sizes
    named = {
        "wanted": pltpu.VMEM((n_row, 1, LANE), jnp.int32),
        "id_send": pltpu.SemaphoreType.DMA((n_row,)),
        "id_recv": pltpu.SemaphoreType.DMA((n_row,)),
        "high": pltpu.VMEM((capacity, block, block), bf16),
        "middle": pltpu.VMEM((capacity, block, block), bf16),
        "low": pltpu.VMEM((capacity, block, block), bf16),
        "columns": pltpu.VMEM((per_owner, width, LANE), f32),
        "held": pltpu.VMEM((2, width, LANE), f32),
        "work": pltpu.VMEM((width, LANE), f32),
    }
    for tag in ("gram_one_", "gram_cols_", "gram_two_"):
        named.update(gram_scratch(sizes, tag))
    named.update(spread_scratch(n_row, chunks, width, "one_"))
    named.update(spread_scratch(n_row, chunks, width, "two_"))
    named.update(row_scratch(n_col, capacity, chunks, width, "one_", True))
    named.update(row_scratch(n_col, capacity, chunks, width, "two_", False))
    named.update(column_scratch(n_row, capacity, chunks, width))
    return named


def factor(gram_ref, count):
    packed = gram_ref[...].reshape(32, LANE)
    lane = lax.broadcasted_iota(jnp.int32, (8, LANE), 1)
    sub = lax.broadcasted_iota(jnp.int32, (8, LANE), 0)
    turned = pltpu.roll(packed, 64, 1)
    groups = []
    for g in range(8):
        source = packed if g < 4 else turned
        h = g % 4
        left = source[h * 8 : (h + 1) * 8] * (1.0 / count)
        ident = jnp.where(lane - 64 == sub + g * 8, 1.0, 0.0).astype(f32)
        groups.append(jnp.where(lane < 64, left, ident))
    pivots = []
    for kb in range(8):
        below = range(kb, 8)
        cols = [
            {g: jnp.broadcast_to(groups[g][:, 8 * kb + i : 8 * kb + i + 1], (8, LANE)) for g in below}
            for i in range(8)
        ]
        lines = [jnp.broadcast_to(groups[kb][i : i + 1, :], (8, LANE)) for i in range(8)]
        scaled = []
        diagonal = jnp.ones((8, LANE), f32)
        for i in range(8):
            pivot = jnp.broadcast_to(cols[i][kb][i : i + 1, :], (8, LANE))
            diagonal = jnp.where(sub == i, pivot, diagonal)
            inverse = 1.0 / pivot
            scaled.append(lines[i] * inverse)
            for j in range(i + 1, 8):
                ratio = jnp.broadcast_to(cols[i][kb][j : j + 1, :], (8, LANE)) * inverse
                lines[j] = lines[j] - ratio * lines[i]
                for g in below:
                    cols[j][g] = cols[j][g] - cols[i][g] * ratio
        block = lines[0]
        for i in range(1, 8):
            block = jnp.where(sub == i, lines[i], block)
        groups[kb] = block
        pivots.append(diagonal)
        for g in range(kb + 1, 8):
            for i in range(8):
                groups[g] = groups[g] - cols[i][g] * scaled[i]
    return [groups[g] / jnp.sqrt(pivots[g]) for g in range(8)]


def split_factor(groups):
    both = jnp.concatenate(groups, axis=0)
    lane = lax.broadcasted_iota(jnp.int32, both.shape, 1)
    sub = lax.broadcasted_iota(jnp.int32, both.shape, 0)
    upper = jnp.where((lane < 64) & (lane >= sub), both, 0.0)
    inverse = jnp.where(lane < 64, pltpu.roll(both, 64, 1), 0.0)
    return upper, inverse


def apply_inverse(inverse, block):
    return nn(inverse, jnp.concatenate([block, jnp.zeros_like(block)], axis=0))


def final_kernel(count, gram_ref, held_ref, basis_ref, q_ref, w_ref, r_ref):
    upper, inverse = split_factor(factor(gram_ref, count))
    r_ref[...] = upper[:, :64]
    w_ref[...] = basis_ref[...]
    for b in range(held_ref.shape[0]):
        q_ref[:, b * LANE : (b + 1) * LANE] = apply_inverse(inverse, held_ref[b])


def call(body, outs, ins, scratch=(), smem=0, collective=None):
    vmem = pl.BlockSpec(memory_space=pltpu.VMEM)
    return pl.pallas_call(
        body,
        out_shape=[jax.ShapeDtypeStruct(shape, kind) for shape, kind in outs],
        in_specs=[pl.BlockSpec(memory_space=pltpu.SMEM)] * smem + [vmem] * (len(ins) - smem),
        out_specs=[vmem] * len(outs),
        scratch_shapes=list(scratch),
        compiler_params=pltpu.CompilerParams(
            collective_id=collective,
            has_side_effects=collective is not None,
            vmem_limit_bytes=24 * 1024 * 1024,
        ),
    )(*ins)


def shards(n_row, n_col, nx, tiles, coords, counts, probes):
    sizes = (n_row, n_col, nx)
    capacity, block = tiles.shape[0], tiles.shape[1]
    width, share = probes.shape[0], probes.shape[2]
    per_owner = share // block
    group_blocks = 2 * n_col
    total_rows = group_blocks * n_row * block
    total_cols = share * n_row * n_col
    order = jnp.arange(capacity, dtype=jnp.int32)
    live = order < counts[0]
    place = coords[:, 0] % group_blocks
    col_local = coords[:, 1] % (per_owner * n_row)
    owner = col_local // per_owner
    within = col_local % per_owner

    def latest(keys, wanted, allowed):
        match = (keys[:, None] == wanted[None, :]) & live[:, None] & allowed
        found = jnp.max(jnp.where(match, order[:, None], -1), axis=0)
        return jnp.where(found < 0, capacity, found)

    rows_wanted = jnp.arange(group_blocks, dtype=jnp.int32)
    owners = jnp.arange(n_row, dtype=jnp.int32)
    before = latest(place, place, order[:, None] < order[None, :])
    info = jnp.concatenate(
        [owner, place, before, latest(place, rows_wanted, True), latest(owner, owners, True)]
    ).astype(jnp.int32)
    match = (owner[:, None] == owners[None, :]) & live[:, None]
    ids = jnp.sum(jnp.where(match, within[:, None] + 1, 0), axis=0)
    ids = jnp.broadcast_to(ids[:, None, None], (n_row, 1, LANE)).astype(jnp.int32)

    scratch = whole_scratch(sizes, CHUNKS, capacity, width, per_owner, block)
    held, gram, basis = call(
        functools.partial(whole_kernel, sizes, CHUNKS, (total_rows, total_cols), list(scratch)),
        [((2, width, LANE), f32), ((32, LANE), f32), ((width, share), bf16)],
        (info, tiles, probes.reshape(width, share), ids),
        scratch.values(),
        smem=1,
        collective=0,
    )
    q_basis, w_basis, r_factor = call(
        functools.partial(final_kernel, total_rows),
        [((width, 2 * LANE), f32), ((width, share), bf16), ((width, width), f32)],
        (gram, held, basis),
    )
    return (q_basis, w_basis.reshape(width, 1, share), r_factor)


def solution(mesh):
    n_row, n_col = mesh.shape["row"], mesh.shape["col"]
    nx = 4 if n_row >= 16 else 2
    in_specs = (
        P(("row", "col"), None, None),
        P(("row", "col"), None),
        P(("row", "col")),
        P(None, "col", "row"),
    )
    out_specs = (P(None, ("row", "col")), P(None, "col", "row"), P())
    return jax.shard_map(
        functools.partial(shards, n_row, n_col, nx),
        mesh=mesh,
        in_specs=in_specs,
        out_specs=out_specs,
        check_vma=False,
    )
```

```python
import functools

import jax
import jax.numpy as jnp
from jax import lax
from jax.experimental import pallas as pl
from jax.experimental.pallas import tpu as pltpu
from jax.sharding import PartitionSpec as P

MESH = pl.DeviceIdType.MESH
highest = lax.Precision.HIGHEST
f32 = jnp.float32
bf16 = jnp.bfloat16
LANE = 128
CORES = 2
CHUNKS = 4
TOGETHER = 4


def nn(left, right):
    return lax.dot_general(
        left, right, (((1,), (0,)), ((), ())), precision=highest, preferred_element_type=f32
    )


def nt(left, right):
    return lax.dot_general(
        left, right, (((1,), (1,)), ((), ())), precision=highest, preferred_element_type=f32
    )


def remote(src, dst, send, recv, device):
    return pltpu.make_async_remote_copy(
        src_ref=src,
        dst_ref=dst,
        send_sem=send,
        recv_sem=recv,
        device_id=device,
        device_id_type=MESH,
    )


def loop(lower, upper, body):
    def step(i, carry):
        body(i)
        return carry

    lax.fori_loop(lower, upper, step, 0)


def offset(k, n):
    step = (k + 1) // 2
    return n // 2 + step * (2 * lax.rem(k, 2) - 1)


def greet(n_row, n_col, row, col, with_row, with_col):
    barrier = pltpu.get_barrier_semaphore()
    count = 0
    if with_row:
        loop(
            1,
            n_row,
            lambda d: pl.semaphore_signal(
                barrier, inc=1, device_id=(lax.rem(row + d, n_row), col), device_id_type=MESH
            ),
        )
        count += n_row - 1
    if with_col:
        loop(
            1,
            n_col,
            lambda d: pl.semaphore_signal(
                barrier, inc=1, device_id=(row, lax.rem(col + d, n_col)), device_id_type=MESH
            ),
        )
        count += n_col - 1
    pl.semaphore_wait(barrier, count)


class Exchange:
    def __init__(self, n, me, source, dst, send, recv, device):
        self.n, self.me, self.source, self.dst = n, me, source, dst
        self.send, self.recv, self.device = send, recv, device

    def copy_to(self, peer):
        return remote(
            self.source(peer),
            self.dst.at[self.me],
            self.send.at[peer],
            self.recv.at[self.me],
            self.device(peer),
        )

    def copy_from(self, peer):
        return remote(
            self.source(peer),
            self.dst.at[peer],
            self.send.at[peer],
            self.recv.at[peer],
            self.device(peer),
        )

    def start(self):
        loop(
            0, self.n - 1, lambda k: self.copy_to(lax.rem(self.me + offset(k, self.n), self.n)).start()
        )

    def wait(self):
        loop(
            0,
            self.n - 1,
            lambda k: self.copy_from(lax.rem(self.me - offset(k, self.n) + self.n, self.n)).wait(),
        )


def sum_slots(ref, n):
    total = ref[0]
    for s in range(1, n):
        total = total + ref[s]
    return total


def pack_gram(block):
    size = block.shape[0]
    half = size // 2
    zero = jnp.zeros_like(block)
    return nt(block[:half], jnp.concatenate([block, zero], axis=0)) + nt(
        block[half:], jnp.concatenate([zero, block], axis=0)
    )


class GramSum:
    def __init__(self, sizes, row, col, r, tag):
        n_row, n_col, nx = sizes
        nz = n_row // nx
        z, x = row // nx, lax.rem(row, nx)
        self.nx, self.nz, self.nc, self.x, self.z, self.col = nx, nz, n_col, x, z, col
        get = lambda name: r[tag + name]
        self.part, self.gx, self.s1, self.gz = get("part"), get("gx"), get("s1"), get("gz")
        self.s2, self.gc, self.out = get("s2"), get("gc"), get("out")
        along_x = lambda p: (z * nx + p, col)
        along_z = lambda p: (p * nx + x, col)
        along_c = lambda p: (row, p)
        part, s1, s2, out = self.part, self.s1, self.s2, self.out
        self.first = Exchange(
            nx, x, lambda p: part.at[p], self.gx, get("x_send"), get("x_recv"), along_x
        )
        self.second = Exchange(nz, z, lambda p: s1, self.gz, get("z_send"), get("z_recv"), along_z)
        self.third = Exchange(
            n_col, col, lambda p: s2, self.gc, get("c_send"), get("c_recv"), along_c
        )
        self.last = Exchange(
            nx, x, lambda p: out.at[x], out, get("o_send"), get("o_recv"), along_x
        )

    def scatter_x(self, packed):
        depth = packed.shape[0] // self.nx
        for j in range(self.nx):
            self.part[j] = packed[j * depth : (j + 1) * depth]
        self.first.start()
        self.gx[self.x] = self.part[self.x]

    def sum_z(self):
        self.first.wait()
        self.s1[...] = sum_slots(self.gx, self.nx)
        self.second.start()
        self.gz[self.z] = self.s1[...]

    def sum_columns(self):
        self.second.wait()
        self.s2[...] = sum_slots(self.gz, self.nz)
        self.third.start()
        self.gc[self.col] = self.s2[...]

    def gather_x(self):
        self.third.wait()
        self.out[self.x] = sum_slots(self.gc, self.nc)
        self.last.start()

    def result(self):
        self.last.wait()
        return self.out[...].reshape(32, LANE)


def gram_scratch(sizes, tag):
    n_row, n_col, nx = sizes
    depth = 32 // nx
    nz = n_row // nx
    dma = pltpu.SemaphoreType.DMA
    named = {
        "part": pltpu.VMEM((nx, depth, LANE), f32),
        "gx": pltpu.VMEM((nx, depth, LANE), f32),
        "s1": pltpu.VMEM((depth, LANE), f32),
        "gz": pltpu.VMEM((nz, depth, LANE), f32),
        "s2": pltpu.VMEM((depth, LANE), f32),
        "gc": pltpu.VMEM((n_col, depth, LANE), f32),
        "out": pltpu.VMEM((nx, depth, LANE), f32),
        "x_send": dma((nx,)),
        "x_recv": dma((nx,)),
        "z_send": dma((nz,)),
        "z_recv": dma((nz,)),
        "c_send": dma((n_col,)),
        "c_recv": dma((n_col,)),
        "o_send": dma((nx,)),
        "o_recv": dma((nx,)),
    }
    return {tag + name: shape for name, shape in named.items()}


def pick(own, wanted):
    wanted = jnp.broadcast_to(wanted, (own.shape[0], LANE))
    total = jnp.zeros((own.shape[0], LANE), f32)
    for b in range(own.shape[1] // LANE):
        total = jnp.where(wanted == b + 1, own[:, b * LANE : (b + 1) * LANE].astype(f32), total)
    return total.astype(bf16)


class Spread:
    def __init__(self, n_row, row, col, chunks, r, tag):
        self.n_row, self.row, self.chunks = n_row, row, chunks
        self.wanted = r["wanted"]
        self.outgoing = [r[tag + "outgoing%d" % c] for c in range(chunks)]
        self.got = [r[tag + "got%d" % c] for c in range(chunks)]
        self.moves = [
            Exchange(
                n_row,
                row,
                functools.partial(lambda ref, p: ref.at[p], self.outgoing[c]),
                self.got[c],
                r[tag + "send%d" % c],
                r[tag + "recv%d" % c],
                lambda p: (p, col),
            )
            for c in range(chunks)
        ]

    def store(self, refs, place, block):
        rows = block.shape[0] // self.chunks
        for c in range(self.chunks):
            refs[c][place] = block[c * rows : (c + 1) * rows]

    def start(self, own_ref, ready=None):
        def serve(k):
            peer = lax.rem(self.row - offset(k, self.n_row) + self.n_row, self.n_row)
            if ready is not None:
                ready(peer)
            self.store(self.outgoing, peer, pick(own_ref[...], self.wanted[peer]))
            self.moves[0].copy_to(peer).start()

        loop(0, self.n_row - 1, serve)
        self.store(self.got, self.row, pick(own_ref[...], self.wanted[self.row]))

    def finish(self, c):
        def step(k):
            peer = lax.rem(self.row - offset(k, self.n_row) + self.n_row, self.n_row)
            self.moves[c].copy_from(peer).wait()
            if c + 1 < self.chunks:
                self.moves[c + 1].copy_to(peer).start()

        loop(0, self.n_row - 1, step)


def spread_scratch(n_row, chunks, width, tag):
    rows = width // chunks
    named = {}
    for c in range(chunks):
        named[tag + "outgoing%d" % c] = pltpu.VMEM((n_row, rows, LANE), bf16)
        named[tag + "got%d" % c] = pltpu.VMEM((n_row, rows, LANE), bf16)
        named[tag + "send%d" % c] = pltpu.SemaphoreType.DMA((n_row,))
        named[tag + "recv%d" % c] = pltpu.SemaphoreType.DMA((n_row,))
    return named


class RowSums:
    def __init__(self, n_col, row, col, c, r, tag):
        self.ny = ny = n_col // CORES
        self.n_col = n_col
        self.y, self.core = col // CORES, lax.rem(col, CORES)
        self.row, self.col = row, col
        self.other = col + 1 - 2 * self.core
        get = lambda name: r[tag + name + "%d" % c]
        self.terms, self.part, self.near = get("contrib"), get("rows"), get("near")
        self.near_send, self.near_recv = get("near_send"), get("near_recv")
        self.summed, self.far = get("summed"), get("far")
        self.shares = Exchange(
            ny,
            self.y,
            lambda p: self.summed.at[p],
            self.far,
            get("far_send"),
            get("far_recv"),
            self.same_core,
        )
        if tag + "group%d" % c in r:
            self.group = get("group")
            self.all_send, self.all_recv = get("all_send"), get("all_recv")
            self.pass_send, self.pass_recv = get("pass_send"), get("pass_recv")

    def same_core(self, p):
        return (self.row, p * CORES + self.core)

    def near_copy(self, t):
        return remote(
            self.part.at[t * CORES + (1 - self.core)],
            self.near.at[t],
            self.near_send.at[t],
            self.near_recv.at[t],
            (self.row, self.other),
        )

    def peer(self, k):
        return lax.rem(self.y + offset(k, self.ny), self.ny)

    def sketch(self, got, splits, info):
        capacity = splits[0].shape[0]
        dims = (((1,), (1,)), ((), ()))

        def multiply(t):
            block = got[info["owner"](t)]
            total = lax.dot_general(block, splits[2][t], dims, preferred_element_type=f32)
            total += lax.dot_general(block, splits[1][t], dims, preferred_element_type=f32)
            total += lax.dot_general(block, splits[0][t], dims, preferred_element_type=f32)
            self.terms[t] = total

        each_tile(capacity, multiply)
        self.terms[capacity] = jnp.zeros(self.terms.shape[1:], f32)

        def chain(t):
            self.terms[t] = self.terms[t] + self.terms[info["before"](t)]

        loop(0, capacity, chain)

        def place(p):
            for j in range(2):
                self.part[p, j] = self.terms[info["last"](2 * p + j)]

        loop(0, self.n_col, place)

    def start(self):
        loop(0, self.ny - 1, lambda k: self.near_copy(self.peer(k)).start())
        self.near_copy(self.y).start()

    def pair_up(self):
        def step(k):
            peer = self.peer(k)
            self.near_copy(peer).wait()
            self.summed[peer] = self.part[peer * CORES + self.core] + self.near[peer]
            self.shares.copy_to(peer).start()

        loop(0, self.ny - 1, step)
        self.near_copy(self.y).wait()
        self.far[self.y] = self.part[self.y * CORES + self.core] + self.near[self.y]

    def total(self):
        self.shares.wait()
        return sum_slots(self.far, self.ny)

    def pass_copy(self, slot, peer):
        return remote(
            self.group.at[slot],
            self.group.at[slot],
            self.pass_send.at[peer],
            self.pass_recv.at[peer],
            (self.row, self.other),
        )

    def gather(self, total):
        self.group[self.col] = total
        mine = self.group.at[self.col]

        def send(k):
            peer = self.peer(k)
            remote(
                mine, mine, self.all_send.at[peer], self.all_recv.at[self.y], self.same_core(peer)
            ).start()

        loop(0, self.ny - 1, send)
        self.pass_copy(self.col, self.y).start()

    def gathered(self):
        def relay(k):
            peer = lax.rem(self.y - offset(k, self.ny) + self.ny, self.ny)
            slot = peer * CORES + self.core
            remote(
                self.group.at[self.col],
                self.group.at[slot],
                self.all_send.at[peer],
                self.all_recv.at[peer],
                self.same_core(peer),
            ).wait()
            self.pass_copy(slot, peer).start()

        loop(0, self.ny - 1, relay)
        loop(0, self.ny, lambda p: self.pass_copy(p * CORES + (1 - self.core), p).wait())


def row_scratch(n_col, capacity, chunks, width, tag, gather):
    ny = n_col // CORES
    rows = width // chunks
    dma = pltpu.SemaphoreType.DMA
    named = {}
    for c in range(chunks):
        some = {
            "contrib": pltpu.VMEM((capacity + 1, rows, LANE), f32),
            "rows": pltpu.VMEM((n_col, 2, rows, LANE), f32),
            "near": pltpu.VMEM((ny, 2, rows, LANE), f32),
            "summed": pltpu.VMEM((ny, 2, rows, LANE), f32),
            "far": pltpu.VMEM((ny, 2, rows, LANE), f32),
        }
        sems = ["near_send", "near_recv", "far_send", "far_recv"]
        if gather:
            some["group"] = pltpu.VMEM((n_col, 2, rows, LANE), f32)
            sems += ["all_send", "all_recv", "pass_send", "pass_recv"]
        for name in sems:
            some[name] = dma((ny,))
        for name, shape in some.items():
            named[tag + name + "%d" % c] = shape
    return named


def each_tile(capacity, body):
    def some(q):
        for j in range(TOGETHER):
            body(q * TOGETHER + j)

    loop(0, capacity // TOGETHER, some)


def three(value):
    high = value.astype(bf16)
    rest = value - high.astype(f32)
    middle = rest.astype(bf16)
    return high, middle, (rest - middle.astype(f32)).astype(bf16)


class ColumnSums:
    def __init__(self, n_row, row, col, c, r):
        self.n_row, self.row = n_row, row
        self.terms, self.outgoing, self.arrived = (
            r["terms%d" % c],
            r["leaving%d" % c],
            r["arrived%d" % c],
        )
        self.wanted = r["wanted"]
        self.moved = Exchange(
            n_row,
            row,
            lambda p: self.outgoing.at[p],
            self.arrived,
            r["leaving_send%d" % c],
            r["leaving_recv%d" % c],
            lambda p: (p, col),
        )

    def start(self, group, splits, info):
        capacity = splits[0].shape[0]
        rows = self.terms.shape[1]

        def dot(left, right):
            return lax.dot_general(
                left, right, (((1,), (0,)), ((), ())), preferred_element_type=f32
            )

        def multiply(t):
            place = info["place"](t)
            source = group[place // 2, lax.rem(place, 2)]
            high, middle, low = three(source)
            by_high = dot(jnp.concatenate([high, middle, low], axis=0), splits[0][t])
            by_middle = dot(jnp.concatenate([high, middle], axis=0), splits[1][t])
            by_low = dot(high, splits[2][t])
            small = by_high[2 * rows :] + by_middle[rows:] + by_low
            self.terms[t] = by_high[:rows] + (by_high[rows : 2 * rows] + by_middle[:rows] + small)

        each_tile(capacity, multiply)
        self.terms[capacity] = jnp.zeros(self.terms.shape[1:], f32)

        def serve(k):
            peer = lax.rem(self.row + offset(k, self.n_row), self.n_row)
            self.outgoing[peer] = self.terms[info["slot"](peer)]
            self.moved.copy_to(peer).start()

        loop(0, self.n_row - 1, serve)
        self.arrived[self.row] = self.terms[info["slot"](self.row)]

    def finish(self, columns_ref, first):
        self.moved.wait()
        rows = self.arrived.shape[1]

        def column(b):
            def add(s, total):
                hit = jnp.broadcast_to(self.wanted[s], (rows, LANE)) == b + 1
                return total + jnp.where(hit, self.arrived[s], 0.0)

            columns_ref[b, first : first + rows] = lax.fori_loop(
                0, self.n_row, add, jnp.zeros((rows, LANE), f32)
            )

        loop(0, columns_ref.shape[0], column)


def column_scratch(n_row, capacity, chunks, width):
    rows = width // chunks
    named = {}
    for c in range(chunks):
        named["terms%d" % c] = pltpu.VMEM((capacity + 1, rows, LANE), f32)
        named["leaving%d" % c] = pltpu.VMEM((n_row, rows, LANE), f32)
        named["arrived%d" % c] = pltpu.VMEM((n_row, rows, LANE), f32)
        named["leaving_send%d" % c] = pltpu.SemaphoreType.DMA((n_row,))
        named["leaving_recv%d" % c] = pltpu.SemaphoreType.DMA((n_row,))
    return named


def loop_factor(packed, count, work):
    lane = lax.broadcasted_iota(jnp.int32, (64, LANE), 1)
    line = lax.broadcasted_iota(jnp.int32, (64, LANE), 0)
    sub = lax.broadcasted_iota(jnp.int32, (8, LANE), 0)
    gram = jnp.concatenate([packed, pltpu.roll(packed, 64, 1)], axis=0) * (1.0 / count)
    work[...] = jnp.where(lane < 64, gram, jnp.where(lane - 64 == line, 1.0, 0.0))

    def eliminate(kb):
        base = pl.multiple_of(kb * 8, 8)
        shift = lax.rem(LANE - base, LANE)
        block = work[pl.ds(base, 8), :]
        whole = work[...]
        near = pltpu.roll(block, shift, 1)
        far = pltpu.roll(whole, shift, 1)
        heads = [jnp.broadcast_to(near[:, i : i + 1], (8, LANE)) for i in range(8)]
        cols = [jnp.broadcast_to(far[:, i : i + 1], (64, LANE)) for i in range(8)]
        lines = [jnp.broadcast_to(block[i : i + 1, :], (8, LANE)) for i in range(8)]
        diagonal = jnp.ones((8, LANE), f32)
        total = jnp.zeros((64, LANE), f32)
        final = lines[0]
        for i in range(8):
            pivot = jnp.broadcast_to(heads[i][i : i + 1, :], (8, LANE))
            diagonal = jnp.where(sub == i, pivot, diagonal)
            final = jnp.where(sub == i, lines[i], final)
            inverse = 1.0 / pivot
            scaled = lines[i] * inverse
            total = total + cols[i] * jnp.broadcast_to(scaled[:1], (64, LANE))
            for j in range(i + 1, 8):
                ratio = jnp.broadcast_to(heads[i][j : j + 1, :], (8, LANE)) * inverse
                lines[j] = lines[j] - ratio * lines[i]
                heads[j] = heads[j] - heads[i] * ratio
                cols[j] = cols[j] - cols[i] * jnp.broadcast_to(ratio[:1], (64, LANE))
        work[...] = whole - jnp.where(line >= base + 8, total, 0.0)
        work[pl.ds(base, 8), :] = final / jnp.sqrt(diagonal)

    loop(0, 8, eliminate)


def inverse_of(work):
    both = work[...]
    lane = lax.broadcasted_iota(jnp.int32, both.shape, 1)
    return jnp.where(lane < 64, pltpu.roll(both, 64, 1), 0.0)


def whole_kernel(sizes, chunks, totals, names, info_ref, ids_ref, tiles_hbm, own_hbm, *refs):
    n_row, n_col, nx = sizes
    total_rows, total_cols = totals
    held_ref, gram_ref, basis_ref = refs[:3]
    r = dict(zip(names, refs[3:]))
    row, col = lax.axis_index("row"), lax.axis_index("col")
    tiles_ref, own_ref = r["tiles"], r["own"]
    load_own = pltpu.make_async_copy(own_hbm, own_ref, r["load_sem"].at[0])
    load_tiles = pltpu.make_async_copy(tiles_hbm, tiles_ref, r["load_sem"].at[1])
    load_own.start()
    load_tiles.start()
    capacity = tiles_ref.shape[0]
    starts = {"owner": 0, "place": capacity, "before": 2 * capacity, "last": 3 * capacity}
    starts["slot"] = 3 * capacity + 2 * n_col
    info = {
        name: functools.partial(lambda first, i: info_ref[first + i], first)
        for name, first in starts.items()
    }
    splits = [r["high"], r["middle"], r["low"]]
    wanted = r["wanted"]
    width = own_ref.shape[0]
    rows = width // chunks
    columns_ref, work, held = r["columns"], r["work"], r["held"]

    greet(n_row, n_col, row, col, True, True)
    ids = Exchange(
        n_row,
        row,
        lambda p: ids_ref.at[p],
        wanted,
        r["id_send"],
        r["id_recv"],
        lambda p: (p, col),
    )
    ids.start()
    wanted[row] = ids_ref[row]

    def split(t):
        for ref, piece in zip(splits, three(tiles_ref[t])):
            ref[t] = piece

    spread = Spread(n_row, row, col, chunks, r, "one_")
    sums = [RowSums(n_col, row, col, c, r, "one_") for c in range(chunks)]
    load_own.wait()
    spread.start(own_ref, lambda peer: ids.copy_from(peer).wait())
    load_tiles.wait()
    loop(0, capacity, split)
    gram_one = GramSum(sizes, row, col, r, "gram_one_")
    moves = [ColumnSums(n_row, row, col, c, r) for c in range(chunks)]

    def gather(c):
        total = sums[c].total()
        sums[c].gather(total)
        held[:, c * rows : (c + 1) * rows] = total

    def send_terms(c):
        sums[c].gathered()
        moves[c].start(sums[c].group, splits, info)

    for c in range(chunks):
        spread.finish(c)
        sums[c].sketch(spread.got[c], splits, info)
        sums[c].start()
        if c >= 1:
            gather(c - 1)
        sums[c].pair_up()
        if c >= 2:
            send_terms(c - 2)
    gather(chunks - 1)
    gram_one.scatter_x(pack_gram(held[0]) + pack_gram(held[1]))
    if chunks >= 2:
        send_terms(chunks - 2)
    gram_one.sum_z()
    sums[chunks - 1].gathered()
    gram_one.sum_columns()
    moves[chunks - 1].start(sums[chunks - 1].group, splits, info)
    gram_one.gather_x()
    loop_factor(gram_one.result(), total_rows, work)
    inverse_one = inverse_of(work)
    for c in range(chunks):
        moves[c].finish(columns_ref, c * rows)

    def normalise(b, packed):
        block = apply_inverse(inverse_one, columns_ref[b])
        columns_ref[b] = block
        return packed + pack_gram(block)

    packed = lax.fori_loop(0, columns_ref.shape[0], normalise, jnp.zeros((32, LANE), f32))
    gram_cols = GramSum(sizes, row, col, r, "gram_cols_")
    gram_cols.scatter_x(packed)
    gram_cols.sum_z()
    gram_cols.sum_columns()
    gram_cols.gather_x()
    loop_factor(gram_cols.result(), total_cols, work)
    inverse_cols = inverse_of(work)
    for b in range(columns_ref.shape[0]):
        basis_ref[:, b * LANE : (b + 1) * LANE] = apply_inverse(inverse_cols, columns_ref[b]).astype(
            bf16
        )

    spread = Spread(n_row, row, col, chunks, r, "two_")
    sums = [RowSums(n_col, row, col, c, r, "two_") for c in range(chunks)]
    spread.start(basis_ref)

    def keep(c):
        held_ref[:, c * rows : (c + 1) * rows] = sums[c].total()

    for c in range(chunks):
        spread.finish(c)
        sums[c].sketch(spread.got[c], splits, info)
        sums[c].start()
        if c >= 2:
            keep(c - 2)
        sums[c].pair_up()
    for c in range(max(chunks - 2, 0), chunks):
        keep(c)
    gram_two = GramSum(sizes, row, col, r, "gram_two_")
    gram_two.scatter_x(pack_gram(held_ref[0]) + pack_gram(held_ref[1]))
    gram_two.sum_z()
    gram_two.sum_columns()
    gram_two.gather_x()
    gram_ref[...] = gram_two.result()


def whole_scratch(sizes, chunks, capacity, width, per_owner, block):
    n_row, n_col, nx = sizes
    named = {
        "tiles": pltpu.VMEM((capacity, block, block), f32),
        "own": pltpu.VMEM((width, per_owner * block), bf16),
        "load_sem": pltpu.SemaphoreType.DMA((2,)),
        "wanted": pltpu.VMEM((n_row, 1, LANE), jnp.int32),
        "id_send": pltpu.SemaphoreType.DMA((n_row,)),
        "id_recv": pltpu.SemaphoreType.DMA((n_row,)),
        "high": pltpu.VMEM((capacity, block, block), bf16),
        "middle": pltpu.VMEM((capacity, block, block), bf16),
        "low": pltpu.VMEM((capacity, block, block), bf16),
        "columns": pltpu.VMEM((per_owner, width, LANE), f32),
        "held": pltpu.VMEM((2, width, LANE), f32),
        "work": pltpu.VMEM((width, LANE), f32),
    }
    for tag in ("gram_one_", "gram_cols_", "gram_two_"):
        named.update(gram_scratch(sizes, tag))
    named.update(spread_scratch(n_row, chunks, width, "one_"))
    named.update(spread_scratch(n_row, chunks, width, "two_"))
    named.update(row_scratch(n_col, capacity, chunks, width, "one_", True))
    named.update(row_scratch(n_col, capacity, chunks, width, "two_", False))
    named.update(column_scratch(n_row, capacity, chunks, width))
    return named


def factor(gram_ref, count):
    packed = gram_ref[...].reshape(32, LANE)
    lane = lax.broadcasted_iota(jnp.int32, (8, LANE), 1)
    sub = lax.broadcasted_iota(jnp.int32, (8, LANE), 0)
    turned = pltpu.roll(packed, 64, 1)
    groups = []
    for g in range(8):
        source = packed if g < 4 else turned
        h = g % 4
        left = source[h * 8 : (h + 1) * 8] * (1.0 / count)
        ident = jnp.where(lane - 64 == sub + g * 8, 1.0, 0.0).astype(f32)
        groups.append(jnp.where(lane < 64, left, ident))
    pivots = []
    for kb in range(8):
        below = range(kb, 8)
        cols = [
            {g: jnp.broadcast_to(groups[g][:, 8 * kb + i : 8 * kb + i + 1], (8, LANE)) for g in below}
            for i in range(8)
        ]
        lines = [jnp.broadcast_to(groups[kb][i : i + 1, :], (8, LANE)) for i in range(8)]
        scaled = []
        diagonal = jnp.ones((8, LANE), f32)
        for i in range(8):
            pivot = jnp.broadcast_to(cols[i][kb][i : i + 1, :], (8, LANE))
            diagonal = jnp.where(sub == i, pivot, diagonal)
            inverse = 1.0 / pivot
            scaled.append(lines[i] * inverse)
            for j in range(i + 1, 8):
                ratio = jnp.broadcast_to(cols[i][kb][j : j + 1, :], (8, LANE)) * inverse
                lines[j] = lines[j] - ratio * lines[i]
                for g in below:
                    cols[j][g] = cols[j][g] - cols[i][g] * ratio
        block = lines[0]
        for i in range(1, 8):
            block = jnp.where(sub == i, lines[i], block)
        groups[kb] = block
        pivots.append(diagonal)
        for g in range(kb + 1, 8):
            for i in range(8):
                groups[g] = groups[g] - cols[i][g] * scaled[i]
    return [groups[g] / jnp.sqrt(pivots[g]) for g in range(8)]


def split_factor(groups):
    both = jnp.concatenate(groups, axis=0)
    lane = lax.broadcasted_iota(jnp.int32, both.shape, 1)
    sub = lax.broadcasted_iota(jnp.int32, both.shape, 0)
    upper = jnp.where((lane < 64) & (lane >= sub), both, 0.0)
    inverse = jnp.where(lane < 64, pltpu.roll(both, 64, 1), 0.0)
    return upper, inverse


def apply_inverse(inverse, block):
    return nn(inverse, jnp.concatenate([block, jnp.zeros_like(block)], axis=0))


def final_kernel(count, gram_ref, held_ref, basis_ref, q_ref, w_ref, r_ref):
    upper, inverse = split_factor(factor(gram_ref, count))
    r_ref[...] = upper[:, :64]
    w_ref[...] = basis_ref[...]
    for b in range(held_ref.shape[0]):
        q_ref[:, b * LANE : (b + 1) * LANE] = apply_inverse(inverse, held_ref[b])


def call(body, outs, ins, scratch=(), smem=0, anywhere=0, collective=None):
    vmem = pl.BlockSpec(memory_space=pltpu.VMEM)
    return pl.pallas_call(
        body,
        out_shape=[jax.ShapeDtypeStruct(shape, kind) for shape, kind in outs],
        in_specs=[pl.BlockSpec(memory_space=pltpu.SMEM)] * smem
        + [vmem] * (len(ins) - smem - anywhere)
        + [pl.BlockSpec(memory_space=pl.ANY)] * anywhere,
        out_specs=[vmem] * len(outs),
        scratch_shapes=list(scratch),
        compiler_params=pltpu.CompilerParams(
            collective_id=collective,
            has_side_effects=collective is not None,
            vmem_limit_bytes=62 * 1024 * 1024,
        ),
    )(*ins)


def shards(n_row, n_col, nx, tiles, coords, counts, probes):
    sizes = (n_row, n_col, nx)
    capacity, block = tiles.shape[0], tiles.shape[1]
    width, share = probes.shape[0], probes.shape[2]
    per_owner = share // block
    group_blocks = 2 * n_col
    total_rows = group_blocks * n_row * block
    total_cols = share * n_row * n_col
    order = jnp.arange(capacity, dtype=jnp.int32)
    live = order < counts[0]
    place = coords[:, 0] % group_blocks
    col_local = coords[:, 1] % (per_owner * n_row)
    owner = col_local // per_owner
    within = col_local % per_owner

    def latest(keys, wanted, allowed):
        match = (keys[:, None] == wanted[None, :]) & live[:, None] & allowed
        found = jnp.max(jnp.where(match, order[:, None], -1), axis=0)
        return jnp.where(found < 0, capacity, found)

    rows_wanted = jnp.arange(group_blocks, dtype=jnp.int32)
    owners = jnp.arange(n_row, dtype=jnp.int32)
    before = latest(place, place, order[:, None] < order[None, :])
    info = jnp.concatenate(
        [owner, place, before, latest(place, rows_wanted, True), latest(owner, owners, True)]
    ).astype(jnp.int32)
    match = (owner[:, None] == owners[None, :]) & live[:, None]
    ids = jnp.sum(jnp.where(match, within[:, None] + 1, 0), axis=0)
    ids = jnp.broadcast_to(ids[:, None, None], (n_row, 1, LANE)).astype(jnp.int32)

    scratch = whole_scratch(sizes, CHUNKS, capacity, width, per_owner, block)
    held, gram, basis = call(
        functools.partial(whole_kernel, sizes, CHUNKS, (total_rows, total_cols), list(scratch)),
        [((2, width, LANE), f32), ((32, LANE), f32), ((width, share), bf16)],
        (info, ids, tiles, probes.reshape(width, share)),
        scratch.values(),
        smem=1,
        anywhere=2,
        collective=0,
    )
    q_basis, w_basis, r_factor = call(
        functools.partial(final_kernel, total_rows),
        [((width, 2 * LANE), f32), ((width, share), bf16), ((width, width), f32)],
        (gram, held, basis),
    )
    return (q_basis, w_basis.reshape(width, 1, share), r_factor)


def solution(mesh):
    n_row, n_col = mesh.shape["row"], mesh.shape["col"]
    nx = 4 if n_row >= 16 else 2
    in_specs = (
        P(("row", "col"), None, None),
        P(("row", "col"), None),
        P(("row", "col")),
        P(None, "col", "row"),
    )
    out_specs = (P(None, ("row", "col")), P(None, "col", "row"), P())
    return jax.shard_map(
        functools.partial(shards, n_row, n_col, nx),
        mesh=mesh,
        in_specs=in_specs,
        out_specs=out_specs,
        check_vma=False,
    )
```

```python
import functools

import jax
import jax.numpy as jnp
from jax import lax
from jax.experimental import pallas as pl
from jax.experimental.pallas import tpu as pltpu
from jax.sharding import PartitionSpec as P

MESH = pl.DeviceIdType.MESH
highest = lax.Precision.HIGHEST
f32 = jnp.float32
bf16 = jnp.bfloat16
LANE = 128
CORES = 2
CHUNKS = 2
TOGETHER = 8


def nn(left, right):
    return lax.dot_general(
        left, right, (((1,), (0,)), ((), ())), precision=highest, preferred_element_type=f32
    )


def nt(left, right):
    return lax.dot_general(
        left, right, (((1,), (1,)), ((), ())), precision=highest, preferred_element_type=f32
    )


def remote(src, dst, send, recv, device):
    return pltpu.make_async_remote_copy(
        src_ref=src,
        dst_ref=dst,
        send_sem=send,
        recv_sem=recv,
        device_id=device,
        device_id_type=MESH,
    )


def loop(lower, upper, body):
    def step(i, carry):
        body(i)
        return carry

    lax.fori_loop(lower, upper, step, 0)


def offset(k, n):
    step = (k + 1) // 2
    return n // 2 + step * (2 * lax.rem(k, 2) - 1)


def greet(sizes, row, col):
    n_row, n_col, nx = sizes
    nz = n_row // nx
    z, x = row // nx, lax.rem(row, nx)
    barrier = pltpu.get_barrier_semaphore()

    def signal(device):
        pl.semaphore_signal(barrier, inc=1, device_id=device, device_id_type=MESH)

    loop(1, nx, lambda d: signal((z * nx + lax.rem(x + d, nx), col)))
    loop(1, nz, lambda d: signal((lax.rem(z + d, nz) * nx + x, col)))
    loop(1, n_col, lambda d: signal((row, lax.rem(col + d, n_col))))
    pl.semaphore_wait(barrier, nx + nz + n_col - 3)


class Exchange:
    def __init__(self, n, me, source, dst, send, recv, device):
        self.n, self.me, self.source, self.dst = n, me, source, dst
        self.send, self.recv, self.device = send, recv, device

    def start_one(self, k):
        peer = lax.rem(self.me + offset(k, self.n), self.n)
        remote(
            self.source(peer), self.dst.at[self.me], self.send, self.recv, self.device(peer)
        ).start()

    def start(self):
        loop(0, self.n - 1, self.start_one)

    def wait(self):
        everything = self.dst.at[pl.ds(0, self.n - 1)]
        device = self.device(lax.rem(self.me + 1, self.n))
        remote(everything, everything, self.send, self.recv, device).wait()


def sum_slots(ref, n):
    total = ref[0]
    for s in range(1, n):
        total = total + ref[s]
    return total


def pack_gram(block):
    size = block.shape[0]
    half = size // 2
    zero = jnp.zeros_like(block)
    return nt(block[:half], jnp.concatenate([block, zero], axis=0)) + nt(
        block[half:], jnp.concatenate([zero, block], axis=0)
    )


class GramSum:
    def __init__(self, sizes, row, col, r, tag):
        n_row, n_col, nx = sizes
        nz = n_row // nx
        z, x = row // nx, lax.rem(row, nx)
        self.nx, self.nz, self.nc, self.x, self.z, self.col = nx, nz, n_col, x, z, col
        get = lambda name: r[tag + name]
        self.part, self.gx, self.s1, self.gz = get("part"), get("gx"), get("s1"), get("gz")
        self.s2, self.gc, self.out = get("s2"), get("gc"), get("out")
        along_x = lambda p: (z * nx + p, col)
        along_z = lambda p: (p * nx + x, col)
        along_c = lambda p: (row, p)
        part, s1, s2, out = self.part, self.s1, self.s2, self.out
        self.first = Exchange(
            nx, x, lambda p: part.at[p], self.gx, get("x_send"), get("x_recv"), along_x
        )
        self.second = Exchange(nz, z, lambda p: s1, self.gz, get("z_send"), get("z_recv"), along_z)
        self.third = Exchange(
            n_col, col, lambda p: s2, self.gc, get("c_send"), get("c_recv"), along_c
        )
        self.last = Exchange(
            nx, x, lambda p: out.at[x], out, get("o_send"), get("o_recv"), along_x
        )

    def scatter_x(self, packed):
        depth = packed.shape[0] // self.nx
        for j in range(self.nx):
            self.part[j] = packed[j * depth : (j + 1) * depth]
        self.first.start()
        self.gx[self.x] = self.part[self.x]

    def sum_z(self):
        self.first.wait()
        self.s1[...] = sum_slots(self.gx, self.nx)
        self.second.start()
        self.gz[self.z] = self.s1[...]

    def sum_columns(self):
        self.second.wait()
        self.s2[...] = sum_slots(self.gz, self.nz)
        self.third.start()
        self.gc[self.col] = self.s2[...]

    def gather_x(self):
        self.third.wait()
        self.out[self.x] = sum_slots(self.gc, self.nc)
        self.last.start()

    def result(self):
        self.last.wait()
        return self.out[...].reshape(32, LANE)


def gram_scratch(sizes, tag):
    n_row, n_col, nx = sizes
    depth = 32 // nx
    nz = n_row // nx
    dma = pltpu.SemaphoreType.DMA
    named = {
        "part": pltpu.VMEM((nx, depth, LANE), f32),
        "gx": pltpu.VMEM((nx, depth, LANE), f32),
        "s1": pltpu.VMEM((depth, LANE), f32),
        "gz": pltpu.VMEM((nz, depth, LANE), f32),
        "s2": pltpu.VMEM((depth, LANE), f32),
        "gc": pltpu.VMEM((n_col, depth, LANE), f32),
        "out": pltpu.VMEM((nx, depth, LANE), f32),
        "x_send": dma,
        "x_recv": dma,
        "z_send": dma,
        "z_recv": dma,
        "c_send": dma,
        "c_recv": dma,
        "o_send": dma,
        "o_recv": dma,
    }
    return {tag + name: shape for name, shape in named.items()}


def pick(own, wanted):
    wanted = jnp.broadcast_to(wanted, (own.shape[0], LANE))
    total = jnp.zeros((own.shape[0], LANE), f32)
    for b in range(own.shape[1] // LANE):
        total = jnp.where(wanted == b + 1, own[:, b * LANE : (b + 1) * LANE].astype(f32), total)
    return total.astype(bf16)


class RowExchange:
    def __init__(self, sizes, row, col, out, r, tag):
        n_row, n_col, nx = sizes
        nz = n_row // nx
        z, x = row // nx, lax.rem(row, nx)
        self.nx, self.nz, self.x, self.z, self.out = nx, nz, x, z, out
        self.mid, self.got = r[tag + "mid"], r[tag + "got"]
        self.along_x = Exchange(
            nx,
            x,
            lambda p: out.at[p],
            None,
            r[tag + "x_send"],
            r[tag + "x_recv"],
            lambda p: (z * nx + p, col),
        )
        self.along_z = Exchange(
            nz,
            z,
            lambda p: self.mid.at[p],
            self.got,
            r[tag + "z_send"],
            r[tag + "z_recv"],
            lambda p: (p * nx + x, col),
        )

    def x_peer(self, k):
        return lax.rem(self.x + offset(k, self.nx), self.nx)

    def send_x(self, k):
        e = self.along_x
        peer = self.x_peer(k)
        remote(
            self.out.at[peer], self.mid.at[:, self.x], e.send, e.recv, e.device(peer)
        ).start()

    def turn(self):
        e = self.along_x
        everything = self.out.at[pl.ds(0, self.nx - 1)]
        remote(everything, everything, e.send, e.recv, e.device(self.x_peer(0))).wait()
        self.along_z.start()
        self.got[self.z] = self.mid[self.z]

    def wait(self):
        self.along_z.wait()


def exchange_scratch(sizes, tag, shape, kind, out=True):
    n_row, n_col, nx = sizes
    nz = n_row // nx
    named = {
        tag + "mid": pltpu.VMEM((nz, nx) + shape, kind),
        tag + "got": pltpu.VMEM((nz, nx) + shape, kind),
    }
    if out:
        named[tag + "out"] = pltpu.VMEM((nx, nz) + shape, kind)
    for name in ("x_send", "x_recv", "z_send", "z_recv"):
        named[tag + name] = pltpu.SemaphoreType.DMA
    return named


class Spread:
    def __init__(self, sizes, row, col, chunks, r, tag):
        tags = [tag + "%d" % c for c in range(chunks)]
        self.chunks, self.wanted = chunks, r["wanted_got"]
        self.moves = [RowExchange(sizes, row, col, r[t + "out"], r, t) for t in tags]
        self.got = [move.got for move in self.moves]

    def start(self, own_ref):
        first = self.moves[0]
        rows = own_ref.shape[0] // self.chunks

        def column(peer, store):
            def one(p):
                block = pick(own_ref[...], self.wanted[p, peer])
                for c in range(self.chunks):
                    store(self.moves[c], p, block[c * rows : (c + 1) * rows])

            loop(0, first.nz, one)

        def away(k):
            peer = first.x_peer(k)

            def store(move, p, block):
                move.out[peer, p] = block

            column(peer, store)
            first.send_x(k)

        def here(move, p, block):
            move.mid[p, move.x] = block

        loop(0, first.nx - 1, away)
        column(first.x, here)
        for c in range(self.chunks):
            if c:
                loop(0, first.nx - 1, self.moves[c].send_x)
        for c in range(self.chunks):
            self.moves[c].turn()


class RowSums:
    def __init__(self, n_col, row, col, c, r, tag):
        self.ny = ny = n_col // CORES
        self.y, self.core = col // CORES, lax.rem(col, CORES)
        self.row = row
        core = self.core
        self.other = (row, col + 1 - 2 * core)
        get = lambda name: r[tag + name + "%d" % c]
        same_core = lambda p: (row, p * CORES + core)
        self.terms, self.part, self.near = get("contrib"), get("rows"), get("near")
        self.near_move = remote(
            self.part.at[1 - core], self.near, get("near_send"), get("near_recv"), self.other
        )
        self.summed, self.far = get("summed"), get("far")
        self.shares = Exchange(
            ny,
            self.y,
            lambda p: self.summed.at[p],
            self.far,
            get("far_send"),
            get("far_recv"),
            same_core,
        )
        if tag + "group%d" % c in r:
            self.group = get("group")
            mine = self.group.at[core]
            self.all_move = Exchange(
                ny,
                self.y,
                lambda p: mine.at[self.y],
                mine,
                get("all_send"),
                get("all_recv"),
                same_core,
            )
            self.pass_move = remote(mine, mine, get("pass_send"), get("pass_recv"), self.other)

    def sketch(self, got, splits, info):
        capacity = splits[0].shape[0]
        dims = (((1,), (1,)), ((), ()))
        nx = got.shape[1]

        def multiply(t):
            owner = info["owner"](t)
            block = got[owner // nx, lax.rem(owner, nx)]
            total = lax.dot_general(block, splits[2][t], dims, preferred_element_type=f32)
            total += lax.dot_general(block, splits[1][t], dims, preferred_element_type=f32)
            total += lax.dot_general(block, splits[0][t], dims, preferred_element_type=f32)
            self.terms[t] = total

        each_tile(capacity, multiply)
        self.terms[capacity] = jnp.zeros(self.terms.shape[1:], f32)

        def chain(t):
            self.terms[t] = self.terms[t] + self.terms[info["before"](t)]

        loop(0, capacity, chain)

        def place(p):
            for core in range(CORES):
                for j in range(2):
                    self.part[core, p, j] = self.terms[info["last"](2 * (CORES * p + core) + j)]

        loop(0, self.ny, place)
        self.near_move.start()

    def pair_up(self):
        self.near_move.wait()

        def step(k):
            peer = lax.rem(self.y + offset(k, self.ny), self.ny)
            self.summed[peer] = self.part[self.core, peer] + self.near[peer]
            self.shares.start_one(k)

        loop(0, self.ny - 1, step)
        self.far[self.y] = self.part[self.core, self.y] + self.near[self.y]

    def total(self):
        self.shares.wait()
        return sum_slots(self.far, self.ny)

    def gather(self, total):
        self.group[self.core, self.y] = total
        self.all_move.start()

    def gathered(self):
        self.all_move.wait()
        self.pass_move.start()
        self.pass_move.wait()


def row_scratch(n_col, capacity, chunks, width, tag, gather):
    ny = n_col // CORES
    rows = width // chunks
    named = {}
    for c in range(chunks):
        some = {
            "contrib": pltpu.VMEM((capacity + 1, rows, LANE), f32),
            "rows": pltpu.VMEM((CORES, ny, 2, rows, LANE), f32),
            "near": pltpu.VMEM((ny, 2, rows, LANE), f32),
            "summed": pltpu.VMEM((ny, 2, rows, LANE), f32),
            "far": pltpu.VMEM((ny, 2, rows, LANE), f32),
        }
        sems = ["near_send", "near_recv", "far_send", "far_recv"]
        if gather:
            some["group"] = pltpu.VMEM((CORES, ny, 2, rows, LANE), f32)
            sems += ["all_send", "all_recv", "pass_send", "pass_recv"]
        for name in sems:
            some[name] = pltpu.SemaphoreType.DMA
        for name, shape in some.items():
            named[tag + name + "%d" % c] = shape
    return named


def each_tile(capacity, body):
    together = min(TOGETHER, capacity)

    def some(q):
        for j in range(together):
            body(q * together + j)

    loop(0, capacity // together, some)


def three(value):
    high = value.astype(bf16)
    rest = value - high.astype(f32)
    middle = rest.astype(bf16)
    return high, middle, (rest - middle.astype(f32)).astype(bf16)


class ColumnSums:
    def __init__(self, sizes, row, col, c, r):
        self.terms, self.wanted = r["terms%d" % c], r["wanted_got"]
        self.move = RowExchange(sizes, row, col, r["sum%dout" % c], r, "sum%d" % c)

    def start(self, group, splits, info):
        capacity = splits[0].shape[0]
        rows = self.terms.shape[1]
        move = self.move

        def dot(left, right):
            return lax.dot_general(
                left, right, (((1,), (0,)), ((), ())), preferred_element_type=f32
            )

        def multiply(t):
            place = info["place"](t)
            source = group[
                lax.rem(place // 2, CORES), place // (2 * CORES), lax.rem(place, 2)
            ]
            high, middle, low = three(source)
            by_high = dot(jnp.concatenate([high, middle, low], axis=0), splits[0][t])
            by_middle = dot(jnp.concatenate([high, middle], axis=0), splits[1][t])
            by_low = dot(high, splits[2][t])
            small = by_high[2 * rows :] + by_middle[rows:] + by_low
            self.terms[t] = by_high[:rows] + (by_high[rows : 2 * rows] + by_middle[:rows] + small)

        each_tile(capacity, multiply)
        self.terms[capacity] = jnp.zeros(self.terms.shape[1:], f32)

        def away(k):
            peer = move.x_peer(k)

            def one(p):
                move.out[peer, p] = self.terms[info["slot"](p * move.nx + peer)]

            loop(0, move.nz, one)
            move.send_x(k)

        def here(p):
            move.mid[p, move.x] = self.terms[info["slot"](p * move.nx + move.x)]

        loop(0, move.nx - 1, away)
        loop(0, move.nz, here)

    def finish(self, columns_ref, first):
        move = self.move
        move.wait()
        rows = self.terms.shape[1]

        def column(b):
            def add(p, total):
                for q in range(move.nx):
                    hit = jnp.broadcast_to(self.wanted[p, q], (rows, LANE)) == b + 1
                    total = total + jnp.where(hit, move.got[p, q], 0.0)
                return total

            columns_ref[b, first : first + rows] = lax.fori_loop(
                0, move.nz, add, jnp.zeros((rows, LANE), f32)
            )

        loop(0, columns_ref.shape[0], column)


def loop_factor(packed, count, work):
    lane = lax.broadcasted_iota(jnp.int32, (64, LANE), 1)
    line = lax.broadcasted_iota(jnp.int32, (64, LANE), 0)
    sub = lax.broadcasted_iota(jnp.int32, (8, LANE), 0)
    gram = jnp.concatenate([packed, pltpu.roll(packed, 64, 1)], axis=0) * (1.0 / count)
    work[...] = jnp.where(lane < 64, gram, jnp.where(lane - 64 == line, 1.0, 0.0))

    def eliminate(kb):
        base = pl.multiple_of(kb * 8, 8)
        shift = lax.rem(LANE - base, LANE)
        block = work[pl.ds(base, 8), :]
        whole = work[...]
        near = pltpu.roll(block, shift, 1)
        far = pltpu.roll(whole, shift, 1)
        heads = [jnp.broadcast_to(near[:, i : i + 1], (8, LANE)) for i in range(8)]
        cols = [jnp.broadcast_to(far[:, i : i + 1], (64, LANE)) for i in range(8)]
        lines = [jnp.broadcast_to(block[i : i + 1, :], (8, LANE)) for i in range(8)]
        diagonal = jnp.ones((8, LANE), f32)
        total = jnp.zeros((64, LANE), f32)
        final = lines[0]
        for i in range(8):
            pivot = jnp.broadcast_to(heads[i][i : i + 1, :], (8, LANE))
            diagonal = jnp.where(sub == i, pivot, diagonal)
            final = jnp.where(sub == i, lines[i], final)
            inverse = 1.0 / pivot
            scaled = lines[i] * inverse
            total = total + cols[i] * jnp.broadcast_to(scaled[:1], (64, LANE))
            for j in range(i + 1, 8):
                ratio = jnp.broadcast_to(heads[i][j : j + 1, :], (8, LANE)) * inverse
                lines[j] = lines[j] - ratio * lines[i]
                heads[j] = heads[j] - heads[i] * ratio
                cols[j] = cols[j] - cols[i] * jnp.broadcast_to(ratio[:1], (64, LANE))
        work[...] = whole - jnp.where(line >= base + 8, total, 0.0)
        work[pl.ds(base, 8), :] = final / jnp.sqrt(diagonal)

    loop(0, 8, eliminate)


def inverse_of(work):
    both = work[...]
    lane = lax.broadcasted_iota(jnp.int32, both.shape, 1)
    return jnp.where(lane < 64, pltpu.roll(both, 64, 1), 0.0)


def whole_kernel(sizes, chunks, totals, names, info_ref, ids_ref, tiles_hbm, own_hbm, *refs):
    n_row, n_col, nx = sizes
    total_rows, total_cols = totals
    held_ref, gram_ref, basis_ref = refs[:3]
    r = dict(zip(names, refs[3:]))
    row, col = lax.axis_index("row"), lax.axis_index("col")
    tiles_ref, own_ref = r["tiles"], r["own"]
    load_own = pltpu.make_async_copy(own_hbm, own_ref, r["load_sem"].at[0])
    load_tiles = pltpu.make_async_copy(tiles_hbm, tiles_ref, r["load_sem"].at[1])
    load_own.start()
    load_tiles.start()
    capacity = tiles_ref.shape[0]
    starts = {"owner": 0, "place": capacity, "before": 2 * capacity, "last": 3 * capacity}
    starts["slot"] = 3 * capacity + 2 * n_col
    info = {
        name: functools.partial(lambda first, i: info_ref[first + i], first)
        for name, first in starts.items()
    }
    splits = [r["high"], r["middle"], r["low"]]
    width = own_ref.shape[0]
    rows = width // chunks
    columns_ref, work, held = r["columns"], r["work"], r["held"]

    greet(sizes, row, col)
    ids = RowExchange(sizes, row, col, ids_ref, r, "wanted_")
    loop(0, nx - 1, ids.send_x)

    def own_id(p):
        ids.mid[p, ids.x] = ids_ref[ids.x, p]

    loop(0, ids.nz, own_id)
    ids.turn()

    def split(t):
        for ref, piece in zip(splits, three(tiles_ref[t])):
            ref[t] = piece

    spread = Spread(sizes, row, col, chunks, r, "one_")
    sums = [RowSums(n_col, row, col, c, r, "one_") for c in range(chunks)]
    load_own.wait()
    ids.wait()
    spread.start(own_ref)
    load_tiles.wait()
    loop(0, capacity, split)
    gram_one = GramSum(sizes, row, col, r, "gram_one_")
    moves = [ColumnSums(sizes, row, col, c, r) for c in range(chunks)]

    def gather(c):
        total = sums[c].total()
        sums[c].gather(total)
        held[:, c * rows : (c + 1) * rows] = total

    def send_terms(c):
        sums[c].gathered()
        moves[c].start(sums[c].group, splits, info)

    for c in range(chunks):
        spread.moves[c].wait()
        sums[c].sketch(spread.got[c], splits, info)
        if c >= 1:
            gather(c - 1)
        sums[c].pair_up()
        if c >= 2:
            send_terms(c - 2)
            moves[c - 2].move.turn()
    last = chunks - 1
    if last >= 1:
        send_terms(last - 1)
    gather(last)
    if last >= 1:
        moves[last - 1].move.turn()
    gram_one.scatter_x(pack_gram(held[0]) + pack_gram(held[1]))
    gram_one.sum_z()
    sums[last].gathered()
    gram_one.sum_columns()
    moves[last].start(sums[last].group, splits, info)
    gram_one.gather_x()
    moves[last].move.turn()
    loop_factor(gram_one.result(), total_rows, work)
    inverse_one = inverse_of(work)
    for c in range(chunks):
        moves[c].finish(columns_ref, c * rows)

    def normalise(b, packed):
        block = apply_inverse(inverse_one, columns_ref[b])
        columns_ref[b] = block
        return packed + pack_gram(block)

    packed = lax.fori_loop(0, columns_ref.shape[0], normalise, jnp.zeros((32, LANE), f32))
    gram_cols = GramSum(sizes, row, col, r, "gram_cols_")
    gram_cols.scatter_x(packed)
    gram_cols.sum_z()
    gram_cols.sum_columns()
    gram_cols.gather_x()
    loop_factor(gram_cols.result(), total_cols, work)
    inverse_cols = inverse_of(work)
    for b in range(columns_ref.shape[0]):
        basis_ref[:, b * LANE : (b + 1) * LANE] = apply_inverse(inverse_cols, columns_ref[b]).astype(
            bf16
        )

    spread = Spread(sizes, row, col, chunks, r, "two_")
    sums = [RowSums(n_col, row, col, c, r, "two_") for c in range(chunks)]
    spread.start(basis_ref)

    def keep(c):
        held_ref[:, c * rows : (c + 1) * rows] = sums[c].total()

    for c in range(chunks):
        spread.moves[c].wait()
        sums[c].sketch(spread.got[c], splits, info)
        if c >= 2:
            keep(c - 2)
        sums[c].pair_up()
    for c in range(max(chunks - 2, 0), chunks):
        keep(c)
    gram_two = GramSum(sizes, row, col, r, "gram_two_")
    gram_two.scatter_x(pack_gram(held_ref[0]) + pack_gram(held_ref[1]))
    gram_two.sum_z()
    gram_two.sum_columns()
    gram_two.gather_x()
    gram_ref[...] = gram_two.result()


def whole_scratch(sizes, chunks, capacity, width, per_owner, block):
    n_row, n_col, nx = sizes
    named = {
        "tiles": pltpu.VMEM((capacity, block, block), f32),
        "own": pltpu.VMEM((width, per_owner * block), bf16),
        "load_sem": pltpu.SemaphoreType.DMA((2,)),
        "high": pltpu.VMEM((capacity, block, block), bf16),
        "middle": pltpu.VMEM((capacity, block, block), bf16),
        "low": pltpu.VMEM((capacity, block, block), bf16),
        "columns": pltpu.VMEM((per_owner, width, LANE), f32),
        "held": pltpu.VMEM((2, width, LANE), f32),
        "work": pltpu.VMEM((width, LANE), f32),
    }
    for tag in ("gram_one_", "gram_cols_", "gram_two_"):
        named.update(gram_scratch(sizes, tag))
    named.update(exchange_scratch(sizes, "wanted_", (1, LANE), jnp.int32, out=False))
    rows = width // chunks
    for c in range(chunks):
        for tag, kind in (("one_", bf16), ("two_", bf16), ("sum", f32)):
            named.update(exchange_scratch(sizes, tag + "%d" % c, (rows, LANE), kind))
        named["terms%d" % c] = pltpu.VMEM((capacity + 1, rows, LANE), f32)
    named.update(row_scratch(n_col, capacity, chunks, width, "one_", True))
    named.update(row_scratch(n_col, capacity, chunks, width, "two_", False))
    return named


def factor(gram_ref, count):
    packed = gram_ref[...].reshape(32, LANE)
    lane = lax.broadcasted_iota(jnp.int32, (8, LANE), 1)
    sub = lax.broadcasted_iota(jnp.int32, (8, LANE), 0)
    turned = pltpu.roll(packed, 64, 1)
    groups = []
    for g in range(8):
        source = packed if g < 4 else turned
        h = g % 4
        left = source[h * 8 : (h + 1) * 8] * (1.0 / count)
        ident = jnp.where(lane - 64 == sub + g * 8, 1.0, 0.0).astype(f32)
        groups.append(jnp.where(lane < 64, left, ident))
    pivots = []
    for kb in range(8):
        below = range(kb, 8)
        cols = [
            {g: jnp.broadcast_to(groups[g][:, 8 * kb + i : 8 * kb + i + 1], (8, LANE)) for g in below}
            for i in range(8)
        ]
        lines = [jnp.broadcast_to(groups[kb][i : i + 1, :], (8, LANE)) for i in range(8)]
        scaled = []
        diagonal = jnp.ones((8, LANE), f32)
        for i in range(8):
            pivot = jnp.broadcast_to(cols[i][kb][i : i + 1, :], (8, LANE))
            diagonal = jnp.where(sub == i, pivot, diagonal)
            inverse = 1.0 / pivot
            scaled.append(lines[i] * inverse)
            for j in range(i + 1, 8):
                ratio = jnp.broadcast_to(cols[i][kb][j : j + 1, :], (8, LANE)) * inverse
                lines[j] = lines[j] - ratio * lines[i]
                for g in below:
                    cols[j][g] = cols[j][g] - cols[i][g] * ratio
        block = lines[0]
        for i in range(1, 8):
            block = jnp.where(sub == i, lines[i], block)
        groups[kb] = block
        pivots.append(diagonal)
        for g in range(kb + 1, 8):
            for i in range(8):
                groups[g] = groups[g] - cols[i][g] * scaled[i]
    return [groups[g] / jnp.sqrt(pivots[g]) for g in range(8)]


def split_factor(groups):
    both = jnp.concatenate(groups, axis=0)
    lane = lax.broadcasted_iota(jnp.int32, both.shape, 1)
    sub = lax.broadcasted_iota(jnp.int32, both.shape, 0)
    upper = jnp.where((lane < 64) & (lane >= sub), both, 0.0)
    inverse = jnp.where(lane < 64, pltpu.roll(both, 64, 1), 0.0)
    return upper, inverse


def apply_inverse(inverse, block):
    return nn(inverse, jnp.concatenate([block, jnp.zeros_like(block)], axis=0))


def final_kernel(count, gram_ref, held_ref, basis_ref, q_ref, w_ref, r_ref):
    upper, inverse = split_factor(factor(gram_ref, count))
    r_ref[...] = upper[:, :64]
    w_ref[...] = basis_ref[...]
    for b in range(held_ref.shape[0]):
        q_ref[:, b * LANE : (b + 1) * LANE] = apply_inverse(inverse, held_ref[b])


def call(body, outs, ins, scratch=(), smem=0, anywhere=0, collective=None):
    vmem = pl.BlockSpec(memory_space=pltpu.VMEM)
    return pl.pallas_call(
        body,
        out_shape=[jax.ShapeDtypeStruct(shape, kind) for shape, kind in outs],
        in_specs=[pl.BlockSpec(memory_space=pltpu.SMEM)] * smem
        + [vmem] * (len(ins) - smem - anywhere)
        + [pl.BlockSpec(memory_space=pl.ANY)] * anywhere,
        out_specs=[vmem] * len(outs),
        scratch_shapes=list(scratch),
        compiler_params=pltpu.CompilerParams(
            collective_id=collective,
            has_side_effects=collective is not None,
            vmem_limit_bytes=62 * 1024 * 1024,
        ),
    )(*ins)


def shards(n_row, n_col, nx, tiles, coords, counts, probes):
    sizes = (n_row, n_col, nx)
    capacity, block = tiles.shape[0], tiles.shape[1]
    width, share = probes.shape[0], probes.shape[2]
    per_owner = share // block
    group_blocks = 2 * n_col
    total_rows = group_blocks * n_row * block
    total_cols = share * n_row * n_col
    order = jnp.arange(capacity, dtype=jnp.int32)
    live = order < counts[0]
    place = coords[:, 0] % group_blocks
    col_local = coords[:, 1] % (per_owner * n_row)
    owner = col_local // per_owner
    within = col_local % per_owner

    def latest(keys, wanted, allowed):
        match = (keys[:, None] == wanted[None, :]) & live[:, None] & allowed
        found = jnp.max(jnp.where(match, order[:, None], -1), axis=0)
        return jnp.where(found < 0, capacity, found)

    rows_wanted = jnp.arange(group_blocks, dtype=jnp.int32)
    owners = jnp.arange(n_row, dtype=jnp.int32)
    before = latest(place, place, order[:, None] < order[None, :])
    info = jnp.concatenate(
        [owner, place, before, latest(place, rows_wanted, True), latest(owner, owners, True)]
    ).astype(jnp.int32)
    match = (owner[:, None] == owners[None, :]) & live[:, None]
    ids = jnp.sum(jnp.where(match, within[:, None] + 1, 0), axis=0)
    ids = ids.reshape(n_row // nx, nx).T
    ids = jnp.broadcast_to(ids[:, :, None, None], ids.shape + (1, LANE)).astype(jnp.int32)

    scratch = whole_scratch(sizes, CHUNKS, capacity, width, per_owner, block)
    held, gram, basis = call(
        functools.partial(whole_kernel, sizes, CHUNKS, (total_rows, total_cols), list(scratch)),
        [((2, width, LANE), f32), ((32, LANE), f32), ((width, share), bf16)],
        (info, ids, tiles, probes.reshape(width, share)),
        scratch.values(),
        smem=1,
        anywhere=2,
        collective=0,
    )
    q_basis, w_basis, r_factor = call(
        functools.partial(final_kernel, total_rows),
        [((width, 2 * LANE), f32), ((width, share), bf16), ((width, width), f32)],
        (gram, held, basis),
    )
    return (q_basis, w_basis.reshape(width, 1, share), r_factor)


def solution(mesh):
    n_row, n_col = mesh.shape["row"], mesh.shape["col"]
    nx = 4 if n_row >= 16 else 2
    in_specs = (
        P(("row", "col"), None, None),
        P(("row", "col"), None),
        P(("row", "col")),
        P(None, "col", "row"),
    )
    out_specs = (P(None, ("row", "col")), P(None, "col", "row"), P())
    return jax.shard_map(
        functools.partial(shards, n_row, n_col, nx),
        mesh=mesh,
        in_specs=in_specs,
        out_specs=out_specs,
        check_vma=False,
    )
```

```python
import functools

import jax
import jax.numpy as jnp
from jax import lax
from jax.experimental import pallas as pl
from jax.experimental.pallas import tpu as pltpu
from jax.sharding import PartitionSpec as P

MESH = pl.DeviceIdType.MESH
highest = lax.Precision.HIGHEST
f32 = jnp.float32
bf16 = jnp.bfloat16
LANE = 128
CORES = 2
CHUNKS = 2
TOGETHER = 16


def nn(left, right):
    return lax.dot_general(
        left, right, (((1,), (0,)), ((), ())), precision=highest, preferred_element_type=f32
    )


def nt(left, right):
    return lax.dot_general(
        left, right, (((1,), (1,)), ((), ())), precision=highest, preferred_element_type=f32
    )


def remote(src, dst, send, recv, device):
    return pltpu.make_async_remote_copy(
        src_ref=src,
        dst_ref=dst,
        send_sem=send,
        recv_sem=recv,
        device_id=device,
        device_id_type=MESH,
    )


def loop(lower, upper, body):
    def step(i, carry):
        body(i)
        return carry

    lax.fori_loop(lower, upper, step, 0)


def offset(k, n):
    step = (k + 1) // 2
    return n // 2 + step * (2 * lax.rem(k, 2) - 1)


def greet(sizes, row, col):
    n_row, n_col, nx = sizes
    barrier = pltpu.get_barrier_semaphore()

    def signal(device):
        pl.semaphore_signal(barrier, inc=1, device_id=device, device_id_type=MESH)

    loop(1, n_row, lambda d: signal((lax.rem(row + d, n_row), col)))
    loop(1, n_col, lambda d: signal((row, lax.rem(col + d, n_col))))
    pl.semaphore_wait(barrier, n_row + n_col - 2)


class Exchange:
    def __init__(self, n, me, source, dst, send, recv, device):
        self.n, self.me, self.source, self.dst = n, me, source, dst
        self.send, self.recv, self.device = send, recv, device

    def start_one(self, k):
        peer = lax.rem(self.me + offset(k, self.n), self.n)
        remote(
            self.source(peer), self.dst.at[self.me], self.send, self.recv, self.device(peer)
        ).start()

    def start(self):
        loop(0, self.n - 1, self.start_one)

    def wait(self):
        if self.n == 1:
            return
        everything = self.dst.at[pl.ds(0, self.n - 1)]
        device = self.device(lax.rem(self.me + 1, self.n))
        remote(everything, everything, self.send, self.recv, device).wait()


def sum_slots(ref, n):
    total = ref[0]
    for s in range(1, n):
        total = total + ref[s]
    return total


def pack_gram(block):
    size = block.shape[0]
    half = size // 2
    zero = jnp.zeros_like(block)
    return nt(block[:half], jnp.concatenate([block, zero], axis=0)) + nt(
        block[half:], jnp.concatenate([zero, block], axis=0)
    )


class GramSum:
    def __init__(self, sizes, row, col, r, tag):
        n_row, n_col, nx = sizes
        nz = n_row // nx
        z, x = row // nx, lax.rem(row, nx)
        self.nx, self.nz, self.nc, self.x, self.z, self.col = nx, nz, n_col, x, z, col
        get = lambda name: r[tag + name]
        self.part, self.gx, self.s1, self.gz = get("part"), get("gx"), get("s1"), get("gz")
        self.s2, self.gc, self.out = get("s2"), get("gc"), get("out")
        along_x = lambda p: (z * nx + p, col)
        along_z = lambda p: (p * nx + x, col)
        along_c = lambda p: (row, p)
        part, s1, s2, out = self.part, self.s1, self.s2, self.out
        self.first = Exchange(
            nx, x, lambda p: part.at[p], self.gx, get("x_send"), get("x_recv"), along_x
        )
        self.second = Exchange(nz, z, lambda p: s1, self.gz, get("z_send"), get("z_recv"), along_z)
        self.third = Exchange(
            n_col, col, lambda p: s2, self.gc, get("c_send"), get("c_recv"), along_c
        )
        self.last = Exchange(
            nx, x, lambda p: out.at[x], out, get("o_send"), get("o_recv"), along_x
        )

    def scatter_x(self, packed):
        depth = packed.shape[0] // self.nx
        for j in range(self.nx):
            self.part[j] = packed[j * depth : (j + 1) * depth]
        self.first.start()
        self.gx[self.x] = self.part[self.x]

    def sum_z(self):
        self.first.wait()
        self.s1[...] = sum_slots(self.gx, self.nx)
        self.second.start()
        self.gz[self.z] = self.s1[...]

    def sum_columns(self):
        self.second.wait()
        self.s2[...] = sum_slots(self.gz, self.nz)
        self.third.start()
        self.gc[self.col] = self.s2[...]

    def gather_x(self):
        self.third.wait()
        self.out[self.x] = sum_slots(self.gc, self.nc)
        self.last.start()

    def result(self):
        self.last.wait()
        return self.out[...].reshape(32, LANE)


def gram_scratch(sizes, tag):
    n_row, n_col, nx = sizes
    depth = 32 // nx
    nz = n_row // nx
    dma = pltpu.SemaphoreType.DMA
    named = {
        "part": pltpu.VMEM((nx, depth, LANE), f32),
        "gx": pltpu.VMEM((nx, depth, LANE), f32),
        "s1": pltpu.VMEM((depth, LANE), f32),
        "gz": pltpu.VMEM((nz, depth, LANE), f32),
        "s2": pltpu.VMEM((depth, LANE), f32),
        "gc": pltpu.VMEM((n_col, depth, LANE), f32),
        "out": pltpu.VMEM((nx, depth, LANE), f32),
        "x_send": dma,
        "x_recv": dma,
        "z_send": dma,
        "z_recv": dma,
        "c_send": dma,
        "c_recv": dma,
        "o_send": dma,
        "o_recv": dma,
    }
    return {tag + name: shape for name, shape in named.items()}


def pick(own, wanted):
    wanted = jnp.broadcast_to(wanted, (own.shape[0], LANE))
    total = jnp.zeros((own.shape[0], LANE), f32)
    for b in range(own.shape[1] // LANE):
        total = jnp.where(wanted == b + 1, own[:, b * LANE : (b + 1) * LANE].astype(f32), total)
    return total.astype(bf16)


class RowExchange:
    def __init__(self, sizes, row, col, out, r, tag):
        n_row, n_col, nx = sizes
        self.n_row, self.nx, self.nz = n_row, nx, n_row // nx
        self.z, self.x, self.row, self.col, self.out = row // nx, lax.rem(row, nx), row, col, out
        self.got, self.send, self.recv = r[tag + "got"], r[tag + "send"], r[tag + "recv"]
        self.relayed = 0
        if tag + "relay_out" in r:
            self.relayed = nx // 2
            self.relay_out, self.relay_in = r[tag + "relay_out"], r[tag + "relay_in"]
            self.relay = remote(
                self.relay_out,
                self.relay_in,
                r[tag + "relay_send"],
                r[tag + "relay_recv"],
                (self.member(self.nz - 1, 0), col),
            )

    def member(self, dz, dx):
        return lax.rem(self.z + dz, self.nz) * self.nx + lax.rem(self.x + dx, self.nx)

    def direct(self, p):
        remote(
            self.out.at[p], self.got.at[self.row], self.send, self.recv, (p, self.col)
        ).start()

    def start(self, store=None):
        nx, nz = self.nx, self.nz
        half = nz // 2

        def serve(p):
            if store is not None:
                store("out", p, p)
            self.direct(p)

        if self.relayed:
            if store is not None:
                for j in range(self.relayed):
                    store("relay_out", j, self.member(half, nx - self.relayed + j))
            self.relay.start()
        loop(0, nx - self.relayed, lambda j: serve(self.member(half, j)))

        def other(k):
            q = k // nx
            distance = half - 1 - q // 2
            ahead = 1 - 2 * lax.rem(q, 2)
            serve(self.member(nz + distance * ahead, lax.rem(k, nx)))

        loop(0, (nz - 2) * nx, other)
        loop(1, nx, lambda j: serve(self.member(0, j)))
        if store is not None:
            store("got", self.row, self.row)

    def forward(self):
        self.relay.wait()
        source = self.member(1, 0)
        for j in range(self.relayed):
            target = self.member(1 + self.nz // 2, self.nx - self.relayed + j)
            remote(
                self.relay_in.at[j], self.got.at[source], self.send, self.recv, (target, self.col)
            ).start()

    def wait(self):
        everything = self.got.at[pl.ds(0, self.n_row - 1)]
        remote(everything, everything, self.send, self.recv, (self.member(1, 0), self.col)).wait()


def exchange_scratch(sizes, tag, shape, kind, plain=False):
    n_row, n_col, nx = sizes
    dma = pltpu.SemaphoreType.DMA
    named = {tag + "got": pltpu.VMEM((n_row,) + shape, kind), tag + "send": dma, tag + "recv": dma}
    if not plain:
        named[tag + "out"] = pltpu.VMEM((n_row,) + shape, kind)
        named[tag + "relay_out"] = pltpu.VMEM((nx // 2,) + shape, kind)
        named[tag + "relay_in"] = pltpu.VMEM((nx // 2,) + shape, kind)
        named[tag + "relay_send"] = dma
        named[tag + "relay_recv"] = dma
    return named


class Spread:
    def __init__(self, sizes, row, col, chunks, r, tag):
        tags = [tag + "%d" % c for c in range(chunks)]
        self.wanted = r["wanted_got"]
        self.moves = [RowExchange(sizes, row, col, r[t + "out"], r, t) for t in tags]
        self.got = [move.got for move in self.moves]

    def start(self, own_ref):
        rows = own_ref.shape[0] // len(self.moves)

        def store(kind, slot, p):
            block = pick(own_ref[...], self.wanted[p])
            for c, move in enumerate(self.moves):
                getattr(move, kind)[slot] = block[c * rows : (c + 1) * rows]

        self.moves[0].start(store)
        for move in self.moves[1:]:
            move.start()
        for move in self.moves:
            move.forward()


class RowSums:
    def __init__(self, n_col, row, col, c, r, tag):
        self.ny = ny = n_col // CORES
        self.y, self.core = col // CORES, lax.rem(col, CORES)
        self.row = row
        core = self.core
        self.other = (row, col + 1 - 2 * core)
        get = lambda name: r[tag + name + "%d" % c]
        same_core = lambda p: (row, p * CORES + core)
        self.terms, self.part, self.near = get("contrib"), get("rows"), get("near")
        self.near_move = remote(
            self.part.at[1 - core], self.near, get("near_send"), get("near_recv"), self.other
        )
        self.summed, self.far = get("summed"), get("far")
        self.shares = Exchange(
            ny,
            self.y,
            lambda p: self.summed.at[p],
            self.far,
            get("far_send"),
            get("far_recv"),
            same_core,
        )
        if tag + "group%d" % c in r:
            self.group = get("group")
            mine = self.group.at[core]
            self.all_move = Exchange(
                ny,
                self.y,
                lambda p: mine.at[self.y],
                mine,
                get("all_send"),
                get("all_recv"),
                same_core,
            )
            self.pass_move = remote(mine, mine, get("pass_send"), get("pass_recv"), self.other)

    def sketch(self, got, splits, info):
        capacity = splits[0].shape[0]
        dims = (((1,), (1,)), ((), ()))

        def multiply(t):
            block = got[info["owner"](t)]
            total = lax.dot_general(block, splits[2][t], dims, preferred_element_type=f32)
            total += lax.dot_general(block, splits[1][t], dims, preferred_element_type=f32)
            total += lax.dot_general(block, splits[0][t], dims, preferred_element_type=f32)
            self.terms[t] = total

        each_tile(capacity, multiply)
        self.terms[capacity] = jnp.zeros(self.terms.shape[1:], f32)

        def chain(t):
            self.terms[t] = self.terms[t] + self.terms[info["before"](t)]

        loop(0, capacity, chain)

        def place(p):
            for core in range(CORES):
                for j in range(2):
                    self.part[core, p, j] = self.terms[info["last"](2 * (CORES * p + core) + j)]

        loop(0, self.ny, place)
        self.near_move.start()

    def pair_up(self):
        self.near_move.wait()

        def step(k):
            peer = lax.rem(self.y + offset(k, self.ny), self.ny)
            self.summed[peer] = self.part[self.core, peer] + self.near[peer]
            self.shares.start_one(k)

        loop(0, self.ny - 1, step)
        self.far[self.y] = self.part[self.core, self.y] + self.near[self.y]

    def total(self):
        self.shares.wait()
        return sum_slots(self.far, self.ny)

    def gather(self, total):
        self.group[self.core, self.y] = total
        self.all_move.start()

    def gathered(self):
        self.all_move.wait()
        self.pass_move.start()
        self.pass_move.wait()


def row_scratch(n_col, capacity, chunks, width, tag, gather):
    ny = n_col // CORES
    rows = width // chunks
    named = {}
    for c in range(chunks):
        some = {
            "contrib": pltpu.VMEM((capacity + 1, rows, LANE), f32),
            "rows": pltpu.VMEM((CORES, ny, 2, rows, LANE), f32),
            "near": pltpu.VMEM((ny, 2, rows, LANE), f32),
            "summed": pltpu.VMEM((ny, 2, rows, LANE), f32),
            "far": pltpu.VMEM((ny, 2, rows, LANE), f32),
        }
        sems = ["near_send", "near_recv", "far_send", "far_recv"]
        if gather:
            some["group"] = pltpu.VMEM((CORES, ny, 2, rows, LANE), f32)
            sems += ["all_send", "all_recv", "pass_send", "pass_recv"]
        for name in sems:
            some[name] = pltpu.SemaphoreType.DMA
        for name, shape in some.items():
            named[tag + name + "%d" % c] = shape
    return named


def each_tile(capacity, body):
    together = min(TOGETHER, capacity)

    def some(q):
        for j in range(together):
            body(q * together + j)

    loop(0, capacity // together, some)


def three(value):
    high = value.astype(bf16)
    rest = value - high.astype(f32)
    middle = rest.astype(bf16)
    return high, middle, (rest - middle.astype(f32)).astype(bf16)


class ColumnSums:
    def __init__(self, sizes, row, col, c, r):
        self.terms, self.wanted = r["terms%d" % c], r["wanted_got"]
        self.move = RowExchange(sizes, row, col, r["sum%dout" % c], r, "sum%d" % c)

    def start(self, group, splits, info):
        capacity = splits[0].shape[0]
        rows = self.terms.shape[1]
        move = self.move

        def dot(left, right):
            return lax.dot_general(
                left, right, (((1,), (0,)), ((), ())), preferred_element_type=f32
            )

        def multiply(t):
            place = info["place"](t)
            source = group[
                lax.rem(place // 2, CORES), place // (2 * CORES), lax.rem(place, 2)
            ]
            high, middle, low = three(source)
            by_high = dot(jnp.concatenate([high, middle, low], axis=0), splits[0][t])
            by_middle = dot(jnp.concatenate([high, middle], axis=0), splits[1][t])
            by_low = dot(high, splits[2][t])
            small = by_high[2 * rows :] + by_middle[rows:] + by_low
            self.terms[t] = by_high[:rows] + (by_high[rows : 2 * rows] + by_middle[:rows] + small)

        each_tile(capacity, multiply)
        self.terms[capacity] = jnp.zeros(self.terms.shape[1:], f32)

        def store(kind, slot, p):
            getattr(move, kind)[slot] = self.terms[info["slot"](p)]

        move.start(store)

    def finish(self, columns_ref, first):
        move = self.move
        move.wait()
        rows = self.terms.shape[1]

        def column(b):
            def add(q, total):
                for j in range(4):
                    p = 4 * q + j
                    hit = jnp.broadcast_to(self.wanted[p], (rows, LANE)) == b + 1
                    total = total + jnp.where(hit, move.got[p], 0.0)
                return total

            columns_ref[b, first : first + rows] = lax.fori_loop(
                0, move.n_row // 4, add, jnp.zeros((rows, LANE), f32)
            )

        loop(0, columns_ref.shape[0], column)


def loop_factor(packed, count, work):
    lane = lax.broadcasted_iota(jnp.int32, (64, LANE), 1)
    line = lax.broadcasted_iota(jnp.int32, (64, LANE), 0)
    sub = lax.broadcasted_iota(jnp.int32, (8, LANE), 0)
    gram = jnp.concatenate([packed, pltpu.roll(packed, 64, 1)], axis=0) * (1.0 / count)
    work[...] = jnp.where(lane < 64, gram, jnp.where(lane - 64 == line, 1.0, 0.0))

    def eliminate(kb):
        base = pl.multiple_of(kb * 8, 8)
        shift = lax.rem(LANE - base, LANE)
        block = work[pl.ds(base, 8), :]
        whole = work[...]
        near = pltpu.roll(block, shift, 1)
        far = pltpu.roll(whole, shift, 1)
        heads = [jnp.broadcast_to(near[:, i : i + 1], (8, LANE)) for i in range(8)]
        cols = [jnp.broadcast_to(far[:, i : i + 1], (64, LANE)) for i in range(8)]
        lines = [jnp.broadcast_to(block[i : i + 1, :], (8, LANE)) for i in range(8)]
        diagonal = jnp.ones((8, LANE), f32)
        total = jnp.zeros((64, LANE), f32)
        final = lines[0]
        for i in range(8):
            pivot = jnp.broadcast_to(heads[i][i : i + 1, :], (8, LANE))
            diagonal = jnp.where(sub == i, pivot, diagonal)
            final = jnp.where(sub == i, lines[i], final)
            inverse = 1.0 / pivot
            scaled = lines[i] * inverse
            total = total + cols[i] * jnp.broadcast_to(scaled[:1], (64, LANE))
            for j in range(i + 1, 8):
                ratio = jnp.broadcast_to(heads[i][j : j + 1, :], (8, LANE)) * inverse
                lines[j] = lines[j] - ratio * lines[i]
                heads[j] = heads[j] - heads[i] * ratio
                cols[j] = cols[j] - cols[i] * jnp.broadcast_to(ratio[:1], (64, LANE))
        work[...] = whole - jnp.where(line >= base + 8, total, 0.0)
        work[pl.ds(base, 8), :] = final / jnp.sqrt(diagonal)

    loop(0, 8, eliminate)


def inverse_of(work):
    both = work[...]
    lane = lax.broadcasted_iota(jnp.int32, both.shape, 1)
    return jnp.where(lane < 64, pltpu.roll(both, 64, 1), 0.0)


def whole_kernel(sizes, chunks, totals, names, info_ref, ids_ref, tiles_hbm, own_hbm, *refs):
    n_row, n_col, nx = sizes
    total_rows, total_cols = totals
    held_ref, gram_ref, basis_ref = refs[:3]
    r = dict(zip(names, refs[3:]))
    row, col = lax.axis_index("row"), lax.axis_index("col")
    tiles_ref, own_ref = r["tiles"], r["own"]
    load_own = pltpu.make_async_copy(own_hbm, own_ref, r["load_sem"].at[0])
    load_tiles = pltpu.make_async_copy(tiles_hbm, tiles_ref, r["load_sem"].at[1])
    load_own.start()
    load_tiles.start()
    capacity = tiles_ref.shape[0]
    starts = {"owner": 0, "place": capacity, "before": 2 * capacity, "last": 3 * capacity}
    starts["slot"] = 3 * capacity + 2 * n_col
    info = {
        name: functools.partial(lambda first, i: info_ref[first + i], first)
        for name, first in starts.items()
    }
    splits = [r["high"], r["middle"], r["low"]]
    width = own_ref.shape[0]
    rows = width // chunks
    columns_ref, work, held = r["columns"], r["work"], r["held"]

    greet(sizes, row, col)
    ids = RowExchange(sizes, row, col, ids_ref, r, "wanted_")
    ids.start()
    ids.got[row] = ids_ref[row]

    def split(t):
        for ref, piece in zip(splits, three(tiles_ref[t])):
            ref[t] = piece

    spread = Spread(sizes, row, col, chunks, r, "one_")
    sums = [RowSums(n_col, row, col, c, r, "one_") for c in range(chunks)]
    load_own.wait()
    ids.wait()
    spread.start(own_ref)
    load_tiles.wait()
    loop(0, capacity, split)
    gram_one = GramSum(sizes, row, col, r, "gram_one_")
    moves = [ColumnSums(sizes, row, col, c, r) for c in range(chunks)]

    def gather(c):
        total = sums[c].total()
        sums[c].gather(total)
        held[:, c * rows : (c + 1) * rows] = total

    def send_terms(c):
        sums[c].gathered()
        moves[c].start(sums[c].group, splits, info)

    for c in range(chunks):
        spread.moves[c].wait()
        sums[c].sketch(spread.got[c], splits, info)
        if c >= 1:
            gather(c - 1)
        sums[c].pair_up()
        if c >= 2:
            send_terms(c - 2)
            moves[c - 2].move.forward()
    last = chunks - 1
    if last >= 1:
        send_terms(last - 1)
    gather(last)
    if last >= 1:
        moves[last - 1].move.forward()
    gram_one.scatter_x(pack_gram(held[0]) + pack_gram(held[1]))
    gram_one.sum_z()
    sums[last].gathered()
    gram_one.sum_columns()
    moves[last].start(sums[last].group, splits, info)
    moves[last].move.forward()
    gram_one.gather_x()
    loop_factor(gram_one.result(), total_rows, work)
    inverse_one = inverse_of(work)
    for c in range(chunks):
        moves[c].finish(columns_ref, c * rows)

    def normalise(b, packed):
        block = apply_inverse(inverse_one, columns_ref[b])
        columns_ref[b] = block
        return packed + pack_gram(block)

    packed = lax.fori_loop(0, columns_ref.shape[0], normalise, jnp.zeros((32, LANE), f32))
    gram_cols = GramSum(sizes, row, col, r, "gram_cols_")
    gram_cols.scatter_x(packed)
    gram_cols.sum_z()
    gram_cols.sum_columns()
    gram_cols.gather_x()
    loop_factor(gram_cols.result(), total_cols, work)
    inverse_cols = inverse_of(work)
    for b in range(columns_ref.shape[0]):
        basis_ref[:, b * LANE : (b + 1) * LANE] = apply_inverse(inverse_cols, columns_ref[b]).astype(
            bf16
        )

    spread = Spread(sizes, row, col, chunks, r, "two_")
    sums = [RowSums(n_col, row, col, c, r, "two_") for c in range(chunks)]
    spread.start(basis_ref)

    def keep(c):
        held_ref[:, c * rows : (c + 1) * rows] = sums[c].total()

    for c in range(chunks):
        spread.moves[c].wait()
        sums[c].sketch(spread.got[c], splits, info)
        if c >= 2:
            keep(c - 2)
        sums[c].pair_up()
    for c in range(max(chunks - 2, 0), chunks):
        keep(c)
    gram_two = GramSum(sizes, row, col, r, "gram_two_")
    gram_two.scatter_x(pack_gram(held_ref[0]) + pack_gram(held_ref[1]))
    gram_two.sum_z()
    gram_two.sum_columns()
    gram_two.gather_x()
    gram_ref[...] = gram_two.result()


def whole_scratch(sizes, chunks, capacity, width, per_owner, block):
    n_row, n_col, nx = sizes
    named = {
        "tiles": pltpu.VMEM((capacity, block, block), f32),
        "own": pltpu.VMEM((width, per_owner * block), bf16),
        "load_sem": pltpu.SemaphoreType.DMA((2,)),
        "high": pltpu.VMEM((capacity, block, block), bf16),
        "middle": pltpu.VMEM((capacity, block, block), bf16),
        "low": pltpu.VMEM((capacity, block, block), bf16),
        "columns": pltpu.VMEM((per_owner, width, LANE), f32),
        "held": pltpu.VMEM((2, width, LANE), f32),
        "work": pltpu.VMEM((width, LANE), f32),
    }
    for tag in ("gram_one_", "gram_cols_", "gram_two_"):
        named.update(gram_scratch(sizes, tag))
    named.update(exchange_scratch(sizes, "wanted_", (1, LANE), jnp.int32, True))
    rows = width // chunks
    for c in range(chunks):
        for tag, kind in (("one_", bf16), ("two_", bf16), ("sum", f32)):
            named.update(exchange_scratch(sizes, tag + "%d" % c, (rows, LANE), kind))
        named["terms%d" % c] = pltpu.VMEM((capacity + 1, rows, LANE), f32)
    named.update(row_scratch(n_col, capacity, chunks, width, "one_", True))
    named.update(row_scratch(n_col, capacity, chunks, width, "two_", False))
    return named


def factor(gram_ref, count):
    packed = gram_ref[...].reshape(32, LANE)
    lane = lax.broadcasted_iota(jnp.int32, (8, LANE), 1)
    sub = lax.broadcasted_iota(jnp.int32, (8, LANE), 0)
    turned = pltpu.roll(packed, 64, 1)
    groups = []
    for g in range(8):
        source = packed if g < 4 else turned
        h = g % 4
        left = source[h * 8 : (h + 1) * 8] * (1.0 / count)
        ident = jnp.where(lane - 64 == sub + g * 8, 1.0, 0.0).astype(f32)
        groups.append(jnp.where(lane < 64, left, ident))
    pivots = []
    for kb in range(8):
        below = range(kb, 8)
        cols = [
            {g: jnp.broadcast_to(groups[g][:, 8 * kb + i : 8 * kb + i + 1], (8, LANE)) for g in below}
            for i in range(8)
        ]
        lines = [jnp.broadcast_to(groups[kb][i : i + 1, :], (8, LANE)) for i in range(8)]
        scaled = []
        diagonal = jnp.ones((8, LANE), f32)
        for i in range(8):
            pivot = jnp.broadcast_to(cols[i][kb][i : i + 1, :], (8, LANE))
            diagonal = jnp.where(sub == i, pivot, diagonal)
            inverse = 1.0 / pivot
            scaled.append(lines[i] * inverse)
            for j in range(i + 1, 8):
                ratio = jnp.broadcast_to(cols[i][kb][j : j + 1, :], (8, LANE)) * inverse
                lines[j] = lines[j] - ratio * lines[i]
                for g in below:
                    cols[j][g] = cols[j][g] - cols[i][g] * ratio
        block = lines[0]
        for i in range(1, 8):
            block = jnp.where(sub == i, lines[i], block)
        groups[kb] = block
        pivots.append(diagonal)
        for g in range(kb + 1, 8):
            for i in range(8):
                groups[g] = groups[g] - cols[i][g] * scaled[i]
    return [groups[g] / jnp.sqrt(pivots[g]) for g in range(8)]


def split_factor(groups):
    both = jnp.concatenate(groups, axis=0)
    lane = lax.broadcasted_iota(jnp.int32, both.shape, 1)
    sub = lax.broadcasted_iota(jnp.int32, both.shape, 0)
    upper = jnp.where((lane < 64) & (lane >= sub), both, 0.0)
    inverse = jnp.where(lane < 64, pltpu.roll(both, 64, 1), 0.0)
    return upper, inverse


def apply_inverse(inverse, block):
    return nn(inverse, jnp.concatenate([block, jnp.zeros_like(block)], axis=0))


def final_kernel(count, gram_ref, held_ref, basis_ref, q_ref, w_ref, r_ref):
    upper, inverse = split_factor(factor(gram_ref, count))
    r_ref[...] = upper[:, :64]
    w_ref[...] = basis_ref[...]
    for b in range(held_ref.shape[0]):
        q_ref[:, b * LANE : (b + 1) * LANE] = apply_inverse(inverse, held_ref[b])


def call(body, outs, ins, scratch=(), smem=0, anywhere=0, collective=None):
    vmem = pl.BlockSpec(memory_space=pltpu.VMEM)
    return pl.pallas_call(
        body,
        out_shape=[jax.ShapeDtypeStruct(shape, kind) for shape, kind in outs],
        in_specs=[pl.BlockSpec(memory_space=pltpu.SMEM)] * smem
        + [vmem] * (len(ins) - smem - anywhere)
        + [pl.BlockSpec(memory_space=pl.ANY)] * anywhere,
        out_specs=[vmem] * len(outs),
        scratch_shapes=list(scratch),
        compiler_params=pltpu.CompilerParams(
            collective_id=collective,
            has_side_effects=collective is not None,
            vmem_limit_bytes=62 * 1024 * 1024,
        ),
    )(*ins)


def shards(n_row, n_col, nx, tiles, coords, counts, probes):
    sizes = (n_row, n_col, nx)
    capacity, block = tiles.shape[0], tiles.shape[1]
    width, share = probes.shape[0], probes.shape[2]
    per_owner = share // block
    group_blocks = 2 * n_col
    total_rows = group_blocks * n_row * block
    total_cols = share * n_row * n_col
    order = jnp.arange(capacity, dtype=jnp.int32)
    live = order < counts[0]
    place = coords[:, 0] % group_blocks
    col_local = coords[:, 1] % (per_owner * n_row)
    owner = col_local // per_owner
    within = col_local % per_owner

    def latest(keys, wanted, allowed):
        match = (keys[:, None] == wanted[None, :]) & live[:, None] & allowed
        found = jnp.max(jnp.where(match, order[:, None], -1), axis=0)
        return jnp.where(found < 0, capacity, found)

    rows_wanted = jnp.arange(group_blocks, dtype=jnp.int32)
    owners = jnp.arange(n_row, dtype=jnp.int32)
    before = latest(place, place, order[:, None] < order[None, :])
    info = jnp.concatenate(
        [owner, place, before, latest(place, rows_wanted, True), latest(owner, owners, True)]
    ).astype(jnp.int32)
    match = (owner[:, None] == owners[None, :]) & live[:, None]
    ids = jnp.sum(jnp.where(match, within[:, None] + 1, 0), axis=0)
    ids = jnp.broadcast_to(ids[:, None, None], (n_row, 1, LANE)).astype(jnp.int32)

    scratch = whole_scratch(sizes, CHUNKS, capacity, width, per_owner, block)
    held, gram, basis = call(
        functools.partial(whole_kernel, sizes, CHUNKS, (total_rows, total_cols), list(scratch)),
        [((2, width, LANE), f32), ((32, LANE), f32), ((width, share), bf16)],
        (info, ids, tiles, probes.reshape(width, share)),
        scratch.values(),
        smem=1,
        anywhere=2,
        collective=0,
    )
    q_basis, w_basis, r_factor = call(
        functools.partial(final_kernel, total_rows),
        [((width, 2 * LANE), f32), ((width, share), bf16), ((width, width), f32)],
        (gram, held, basis),
    )
    return (q_basis, w_basis.reshape(width, 1, share), r_factor)


def solution(mesh):
    n_row, n_col = mesh.shape["row"], mesh.shape["col"]
    nx = 4 if n_row >= 16 else 2
    in_specs = (
        P(("row", "col"), None, None),
        P(("row", "col"), None),
        P(("row", "col")),
        P(None, "col", "row"),
    )
    out_specs = (P(None, ("row", "col")), P(None, "col", "row"), P())
    return jax.shard_map(
        functools.partial(shards, n_row, n_col, nx),
        mesh=mesh,
        in_specs=in_specs,
        out_specs=out_specs,
        check_vma=False,
    )
```

```python
import functools

import jax
import jax.numpy as jnp
from jax import lax
from jax.experimental import pallas as pl
from jax.experimental.pallas import tpu as pltpu
from jax.sharding import PartitionSpec as P

MESH = pl.DeviceIdType.MESH
highest = lax.Precision.HIGHEST
f32 = jnp.float32
bf16 = jnp.bfloat16
LANE = 128
CORES = 2
CHUNKS = 2


def nn(left, right):
    return lax.dot_general(
        left, right, (((1,), (0,)), ((), ())), precision=highest, preferred_element_type=f32
    )


def nt(left, right):
    return lax.dot_general(
        left, right, (((1,), (1,)), ((), ())), precision=highest, preferred_element_type=f32
    )


def remote(src, dst, send, recv, device):
    return pltpu.make_async_remote_copy(
        src_ref=src,
        dst_ref=dst,
        send_sem=send,
        recv_sem=recv,
        device_id=device,
        device_id_type=MESH,
    )


def loop(lower, upper, body):
    def step(i, carry):
        body(i)
        return carry

    lax.fori_loop(lower, upper, step, 0)


def offset(k, n):
    step = (k + 1) // 2
    return n // 2 + step * (2 * lax.rem(k, 2) - 1)


def greet(n_row, n_col, row, col, with_row, with_col):
    barrier = pltpu.get_barrier_semaphore()
    count = 0
    if with_row:
        loop(
            1,
            n_row,
            lambda d: pl.semaphore_signal(
                barrier, inc=1, device_id=(lax.rem(row + d, n_row), col), device_id_type=MESH
            ),
        )
        count += n_row - 1
    if with_col:
        loop(
            1,
            n_col,
            lambda d: pl.semaphore_signal(
                barrier, inc=1, device_id=(row, lax.rem(col + d, n_col)), device_id_type=MESH
            ),
        )
        count += n_col - 1
    pl.semaphore_wait(barrier, count)


class Exchange:
    def __init__(self, n, me, source, dst, send, recv, device, each=False):
        self.n, self.me, self.source, self.dst = n, me, source, dst
        self.send, self.recv, self.device, self.each = send, recv, device, each

    def copy(self, peer, slot):
        send = self.send.at[peer] if self.each else self.send
        recv = self.recv.at[slot] if self.each else self.recv
        return remote(self.source(peer), self.dst.at[slot], send, recv, self.device(peer))

    def copy_to(self, peer):
        return self.copy(peer, self.me)

    def copy_from(self, peer):
        return self.copy(peer, peer)

    def start(self):
        loop(
            0, self.n - 1, lambda k: self.copy_to(lax.rem(self.me + offset(k, self.n), self.n)).start()
        )

    def wait(self):
        if self.n == 1:
            return
        everything = self.dst.at[pl.ds(0, self.n - 1)]
        device = self.device(lax.rem(self.me + 1, self.n))
        remote(everything, everything, self.send, self.recv, device).wait()


def sum_slots(ref, n):
    total = ref[0]
    for s in range(1, n):
        total = total + ref[s]
    return total


def gram_of(block):
    return nt(block, jnp.concatenate([block, jnp.zeros_like(block)], axis=0))


def pack_gram(gram):
    half = gram.shape[0] // 2
    return gram[:half] + pltpu.roll(gram[half:], 64, 1)


class GramSum:
    def __init__(self, sizes, row, col, r, tag):
        n_row, n_col, nx = sizes
        nz = n_row // nx
        z, x = row // nx, lax.rem(row, nx)
        self.nx, self.nz, self.nc, self.x, self.z, self.col = nx, nz, n_col, x, z, col
        get = lambda name: r[tag + name]
        self.part, self.gx, self.s1, self.gz = get("part"), get("gx"), get("s1"), get("gz")
        self.s2, self.gc, self.out = get("s2"), get("gc"), get("out")
        along_x = lambda p: (z * nx + p, col)
        along_z = lambda p: (p * nx + x, col)
        along_c = lambda p: (row, p)
        part, s1, s2, out = self.part, self.s1, self.s2, self.out
        self.first = Exchange(
            nx, x, lambda p: part.at[p], self.gx, get("x_send"), get("x_recv"), along_x
        )
        self.second = Exchange(nz, z, lambda p: s1, self.gz, get("z_send"), get("z_recv"), along_z)
        self.third = Exchange(
            n_col, col, lambda p: s2, self.gc, get("c_send"), get("c_recv"), along_c
        )
        self.last = Exchange(
            nx, x, lambda p: out.at[x], out, get("o_send"), get("o_recv"), along_x
        )

    def scatter_x(self, packed):
        depth = packed.shape[0] // self.nx
        for j in range(self.nx):
            self.part[j] = packed[j * depth : (j + 1) * depth]
        self.first.start()
        self.gx[self.x] = self.part[self.x]

    def sum_z(self):
        self.first.wait()
        self.s1[...] = sum_slots(self.gx, self.nx)
        self.second.start()
        self.gz[self.z] = self.s1[...]

    def sum_columns(self):
        self.second.wait()
        self.s2[...] = sum_slots(self.gz, self.nz)
        self.third.start()
        self.gc[self.col] = self.s2[...]

    def gather_x(self):
        self.third.wait()
        self.out[self.x] = sum_slots(self.gc, self.nc)
        self.last.start()

    def result(self):
        self.last.wait()
        return self.out[...].reshape(32, LANE)


def gram_scratch(sizes, tag):
    n_row, n_col, nx = sizes
    depth = 32 // nx
    nz = n_row // nx
    dma = pltpu.SemaphoreType.DMA
    named = {
        "part": pltpu.VMEM((nx, depth, LANE), f32),
        "gx": pltpu.VMEM((nx, depth, LANE), f32),
        "s1": pltpu.VMEM((depth, LANE), f32),
        "gz": pltpu.VMEM((nz, depth, LANE), f32),
        "s2": pltpu.VMEM((depth, LANE), f32),
        "gc": pltpu.VMEM((n_col, depth, LANE), f32),
        "out": pltpu.VMEM((nx, depth, LANE), f32),
        "x_send": dma,
        "x_recv": dma,
        "z_send": dma,
        "z_recv": dma,
        "c_send": dma,
        "c_recv": dma,
        "o_send": dma,
        "o_recv": dma,
    }
    return {tag + name: shape for name, shape in named.items()}


def pick(own, wanted):
    wanted = jnp.broadcast_to(wanted, (own.shape[0], LANE))
    total = jnp.zeros((own.shape[0], LANE), f32)
    for b in range(own.shape[1] // LANE):
        total = jnp.where(wanted == b + 1, own[:, b * LANE : (b + 1) * LANE].astype(f32), total)
    return total.astype(bf16)


class Spread:
    def __init__(self, n_row, row, col, chunks, r, tag):
        self.n_row, self.row, self.chunks = n_row, row, chunks
        self.wanted = r["wanted"]
        self.outgoing = [r[tag + "outgoing%d" % c] for c in range(chunks)]
        self.got = [r[tag + "got%d" % c] for c in range(chunks)]
        self.moves = [
            Exchange(
                n_row,
                row,
                functools.partial(lambda ref, p: ref.at[p], self.outgoing[c]),
                self.got[c],
                r[tag + "send%d" % c],
                r[tag + "recv%d" % c],
                lambda p: (p, col),
                c + 1 < chunks,
            )
            for c in range(chunks)
        ]

    def store(self, refs, place, block):
        rows = block.shape[0] // self.chunks
        for c in range(self.chunks):
            refs[c][place] = block[c * rows : (c + 1) * rows]

    def start(self, own_ref, ready=None):
        def serve(k):
            peer = lax.rem(self.row - offset(k, self.n_row) + self.n_row, self.n_row)
            if ready is not None:
                ready(peer)
            self.store(self.outgoing, peer, pick(own_ref[...], self.wanted[peer]))
            self.moves[0].copy_to(peer).start()

        loop(0, self.n_row - 1, serve)
        self.store(self.got, self.row, pick(own_ref[...], self.wanted[self.row]))

    def finish(self, c):
        if c + 1 == self.chunks:
            self.moves[c].wait()
            return

        def step(k):
            peer = lax.rem(self.row - offset(k, self.n_row) + self.n_row, self.n_row)
            self.moves[c].copy_from(peer).wait()
            self.moves[c + 1].copy_to(peer).start()

        loop(0, self.n_row - 1, step)


def spread_scratch(n_row, chunks, width, tag):
    rows = width // chunks
    named = {}
    for c in range(chunks):
        named[tag + "outgoing%d" % c] = pltpu.VMEM((n_row, rows, LANE), bf16)
        named[tag + "got%d" % c] = pltpu.VMEM((n_row, rows, LANE), bf16)
        for name in ("send%d", "recv%d"):
            each = pltpu.SemaphoreType.DMA((n_row,))
            named[tag + name % c] = each if c + 1 < chunks else pltpu.SemaphoreType.DMA
    return named


class RowSums:
    def __init__(self, n_col, row, col, c, r, tag):
        self.ny = ny = n_col // CORES
        self.n_col = n_col
        self.y, self.core = col // CORES, lax.rem(col, CORES)
        self.row, self.col = row, col
        self.other = col + 1 - 2 * self.core
        get = lambda name: r[tag + name + "%d" % c]
        self.terms, self.part, self.near = get("contrib"), get("rows"), get("near")
        self.near_send, self.near_recv = get("near_send"), get("near_recv")
        self.summed, self.far = get("summed"), get("far")
        self.shares = Exchange(
            ny,
            self.y,
            lambda p: self.summed.at[p],
            self.far,
            get("far_send"),
            get("far_recv"),
            self.same_core,
        )
        if tag + "group%d" % c in r:
            self.group = get("group")
            self.all_send, self.all_recv = get("all_send"), get("all_recv")
            self.pass_send, self.pass_recv = get("pass_send"), get("pass_recv")

    def same_core(self, p):
        return (self.row, p * CORES + self.core)

    def near_copy(self, t):
        return remote(
            self.part.at[t * CORES + (1 - self.core)],
            self.near.at[t],
            self.near_send.at[t],
            self.near_recv.at[t],
            (self.row, self.other),
        )

    def peer(self, k):
        return lax.rem(self.y + offset(k, self.ny), self.ny)

    def sketch(self, got, splits, info):
        capacity = splits[0].shape[0]
        dims = (((1,), (1,)), ((), ()))
        for t in range(capacity):
            block = got[info["owner"](t)]
            total = lax.dot_general(block, splits[2][t], dims, preferred_element_type=f32)
            total += lax.dot_general(block, splits[1][t], dims, preferred_element_type=f32)
            total += lax.dot_general(block, splits[0][t], dims, preferred_element_type=f32)
            self.terms[t] = total
        self.terms[capacity] = jnp.zeros(self.terms.shape[1:], f32)

        def chain(t):
            self.terms[t] = self.terms[t] + self.terms[info["before"](t)]

        loop(0, capacity, chain)

        def place(p):
            for j in range(2):
                self.part[p, j] = self.terms[info["last"](2 * p + j)]

        loop(0, self.n_col, place)

    def start(self):
        loop(0, self.ny - 1, lambda k: self.near_copy(self.peer(k)).start())
        self.near_copy(self.y).start()

    def pair_up(self):
        def step(k):
            peer = self.peer(k)
            self.near_copy(peer).wait()
            self.summed[peer] = self.part[peer * CORES + self.core] + self.near[peer]
            self.shares.copy_to(peer).start()

        loop(0, self.ny - 1, step)
        self.near_copy(self.y).wait()
        self.far[self.y] = self.part[self.y * CORES + self.core] + self.near[self.y]

    def total(self):
        self.shares.wait()
        return sum_slots(self.far, self.ny)

    def pass_copy(self, slot, peer):
        return remote(
            self.group.at[slot],
            self.group.at[slot],
            self.pass_send.at[peer],
            self.pass_recv.at[peer],
            (self.row, self.other),
        )

    def gather(self, total):
        self.group[self.col] = total
        mine = self.group.at[self.col]

        def send(k):
            peer = self.peer(k)
            remote(
                mine, mine, self.all_send.at[peer], self.all_recv.at[self.y], self.same_core(peer)
            ).start()

        loop(0, self.ny - 1, send)
        self.pass_copy(self.col, self.y).start()

    def gathered(self):
        def relay(k):
            peer = lax.rem(self.y - offset(k, self.ny) + self.ny, self.ny)
            slot = peer * CORES + self.core
            remote(
                self.group.at[self.col],
                self.group.at[slot],
                self.all_send.at[peer],
                self.all_recv.at[peer],
                self.same_core(peer),
            ).wait()
            self.pass_copy(slot, peer).start()

        loop(0, self.ny - 1, relay)
        loop(0, self.ny, lambda p: self.pass_copy(p * CORES + (1 - self.core), p).wait())


def row_scratch(n_col, capacity, chunks, width, tag, gather):
    ny = n_col // CORES
    rows = width // chunks
    dma = pltpu.SemaphoreType.DMA
    named = {}
    for c in range(chunks):
        some = {
            "contrib": pltpu.VMEM((capacity + 1, rows, LANE), f32),
            "rows": pltpu.VMEM((n_col, 2, rows, LANE), f32),
            "near": pltpu.VMEM((ny, 2, rows, LANE), f32),
            "summed": pltpu.VMEM((ny, 2, rows, LANE), f32),
            "far": pltpu.VMEM((ny, 2, rows, LANE), f32),
        }
        some["far_send"] = some["far_recv"] = dma
        sems = ["near_send", "near_recv"]
        if gather:
            some["group"] = pltpu.VMEM((n_col, 2, rows, LANE), f32)
            sems += ["all_send", "all_recv", "pass_send", "pass_recv"]
        for name in sems:
            some[name] = dma((ny,))
        for name, shape in some.items():
            named[tag + name + "%d" % c] = shape
    return named


def three(value):
    high = value.astype(bf16)
    rest = value - high.astype(f32)
    middle = rest.astype(bf16)
    return high, middle, (rest - middle.astype(f32)).astype(bf16)


class ColumnSums:
    def __init__(self, n_row, row, col, c, r):
        self.n_row, self.row = n_row, row
        self.terms, self.outgoing, self.arrived = (
            r["terms%d" % c],
            r["leaving%d" % c],
            r["arrived%d" % c],
        )
        self.wanted = r["wanted"]
        self.moved = Exchange(
            n_row,
            row,
            lambda p: self.outgoing.at[p],
            self.arrived,
            r["leaving_send%d" % c],
            r["leaving_recv%d" % c],
            lambda p: (p, col),
        )

    def start(self, group, splits, info):
        capacity = splits[0].shape[0]
        rows = self.terms.shape[1]

        def dot(left, right):
            return lax.dot_general(
                left, right, (((1,), (0,)), ((), ())), preferred_element_type=f32
            )

        for t in range(capacity):
            place = info["place"](t)
            source = group[place // 2, lax.rem(place, 2)]
            high, middle, low = three(source)
            by_high = dot(jnp.concatenate([high, middle, low], axis=0), splits[0][t])
            by_middle = dot(jnp.concatenate([high, middle], axis=0), splits[1][t])
            by_low = dot(high, splits[2][t])
            small = by_high[2 * rows :] + by_middle[rows:] + by_low
            self.terms[t] = by_high[:rows] + (by_high[rows : 2 * rows] + by_middle[:rows] + small)
        self.terms[capacity] = jnp.zeros(self.terms.shape[1:], f32)

        def serve(k):
            peer = lax.rem(self.row + offset(k, self.n_row), self.n_row)
            self.outgoing[peer] = self.terms[info["slot"](peer)]
            self.moved.copy_to(peer).start()

        loop(0, self.n_row - 1, serve)
        self.arrived[self.row] = self.terms[info["slot"](self.row)]

    def finish(self, columns_ref, first):
        self.moved.wait()
        rows = self.arrived.shape[1]

        def column(b):
            def add(q, total):
                for j in range(8):
                    s = 8 * q + j
                    hit = jnp.broadcast_to(self.wanted[s], (rows, LANE)) == b + 1
                    total = total + jnp.where(hit, self.arrived[s], 0.0)
                return total

            columns_ref[b, first : first + rows] = lax.fori_loop(
                0, self.n_row // 8, add, jnp.zeros((rows, LANE), f32)
            )

        loop(0, columns_ref.shape[0], column)


def column_scratch(n_row, capacity, chunks, width):
    rows = width // chunks
    named = {}
    for c in range(chunks):
        named["terms%d" % c] = pltpu.VMEM((capacity + 1, rows, LANE), f32)
        named["leaving%d" % c] = pltpu.VMEM((n_row, rows, LANE), f32)
        named["arrived%d" % c] = pltpu.VMEM((n_row, rows, LANE), f32)
        named["leaving_send%d" % c] = pltpu.SemaphoreType.DMA
        named["leaving_recv%d" % c] = pltpu.SemaphoreType.DMA
    return named


def loop_factor(packed, count, work):
    lane = lax.broadcasted_iota(jnp.int32, (64, LANE), 1)
    line = lax.broadcasted_iota(jnp.int32, (64, LANE), 0)
    sub = lax.broadcasted_iota(jnp.int32, (8, LANE), 0)
    gram = jnp.concatenate([packed, pltpu.roll(packed, 64, 1)], axis=0) * (1.0 / count)
    work[...] = jnp.where(lane < 64, gram, jnp.where(lane - 64 == line, 1.0, 0.0))

    def eliminate(kb):
        base = pl.multiple_of(kb * 8, 8)
        shift = lax.rem(LANE - base, LANE)
        block = work[pl.ds(base, 8), :]
        whole = work[...]
        near = pltpu.roll(block, shift, 1)
        far = pltpu.roll(whole, shift, 1)
        heads = [jnp.broadcast_to(near[:, i : i + 1], (8, LANE)) for i in range(8)]
        cols = [jnp.broadcast_to(far[:, i : i + 1], (64, LANE)) for i in range(8)]
        lines = [jnp.broadcast_to(block[i : i + 1, :], (8, LANE)) for i in range(8)]
        diagonal = jnp.ones((8, LANE), f32)
        total = jnp.zeros((64, LANE), f32)
        final = lines[0]
        for i in range(8):
            pivot = jnp.broadcast_to(heads[i][i : i + 1, :], (8, LANE))
            diagonal = jnp.where(sub == i, pivot, diagonal)
            final = jnp.where(sub == i, lines[i], final)
            inverse = 1.0 / pivot
            scaled = lines[i] * inverse
            total = total + cols[i] * jnp.broadcast_to(scaled[:1], (64, LANE))
            for j in range(i + 1, 8):
                ratio = jnp.broadcast_to(heads[i][j : j + 1, :], (8, LANE)) * inverse
                lines[j] = lines[j] - ratio * lines[i]
                heads[j] = heads[j] - heads[i] * ratio
                cols[j] = cols[j] - cols[i] * jnp.broadcast_to(ratio[:1], (64, LANE))
        work[...] = whole - jnp.where(line >= base + 8, total, 0.0)
        work[pl.ds(base, 8), :] = final / jnp.sqrt(diagonal)

    loop(0, 8, eliminate)


def inverse_of(work):
    both = work[...]
    lane = lax.broadcasted_iota(jnp.int32, both.shape, 1)
    return jnp.where(lane < 64, pltpu.roll(both, 64, 1), 0.0)


def whole_kernel(sizes, chunks, totals, names, info_ref, tiles_ref, own_ref, ids_ref, *refs):
    n_row, n_col, nx = sizes
    total_rows, total_cols = totals
    held_ref, gram_ref, basis_ref = refs[:3]
    r = dict(zip(names, refs[3:]))
    row, col = lax.axis_index("row"), lax.axis_index("col")
    capacity = tiles_ref.shape[0]
    starts = {"owner": 0, "place": capacity, "before": 2 * capacity, "last": 3 * capacity}
    starts["slot"] = 3 * capacity + 2 * n_col
    info = {
        name: functools.partial(lambda first, i: info_ref[first + i], first)
        for name, first in starts.items()
    }
    splits = [r["high"], r["middle"], r["low"]]
    wanted = r["wanted"]
    width = own_ref.shape[0]
    rows = width // chunks
    columns_ref, work, held = r["columns"], r["work"], r["held"]

    greet(n_row, n_col, row, col, True, True)
    ids = Exchange(
        n_row,
        row,
        lambda p: ids_ref.at[p],
        wanted,
        r["id_send"],
        r["id_recv"],
        lambda p: (p, col),
        True,
    )
    ids.start()
    wanted[row] = ids_ref[row]

    def split(t):
        for ref, piece in zip(splits, three(tiles_ref[t])):
            ref[t] = piece

    loop(0, capacity, split)

    spread = Spread(n_row, row, col, chunks, r, "one_")
    sums = [RowSums(n_col, row, col, c, r, "one_") for c in range(chunks)]
    spread.start(own_ref, lambda peer: ids.copy_from(peer).wait())
    gram_one = GramSum(sizes, row, col, r, "gram_one_")
    moves = [ColumnSums(n_row, row, col, c, r) for c in range(chunks)]

    def gather(c):
        total = sums[c].total()
        sums[c].gather(total)
        held[:, c * rows : (c + 1) * rows] = total

    def send_terms(c):
        sums[c].gathered()
        moves[c].start(sums[c].group, splits, info)

    for c in range(chunks):
        spread.finish(c)
        sums[c].sketch(spread.got[c], splits, info)
        sums[c].start()
        if c >= 1:
            gather(c - 1)
        sums[c].pair_up()
        if c >= 1:
            send_terms(c - 1)
    last = chunks - 1
    gather(last)
    gram_one.scatter_x(pack_gram(gram_of(held[0]) + gram_of(held[1])))
    gram_one.sum_z()
    gram_one.sum_columns()
    sums[last].gathered()
    gram_one.gather_x()
    moves[last].start(sums[last].group, splits, info)
    loop_factor(gram_one.result(), total_rows, work)
    inverse_one = inverse_of(work)
    for c in range(chunks):
        moves[c].finish(columns_ref, c * rows)

    total = jnp.zeros((width, LANE), f32)
    for b in range(columns_ref.shape[0]):
        block = apply_inverse(inverse_one, columns_ref[b])
        columns_ref[b] = block
        total = total + gram_of(block)
    packed = pack_gram(total)
    gram_cols = GramSum(sizes, row, col, r, "gram_cols_")
    gram_cols.scatter_x(packed)
    gram_cols.sum_z()
    gram_cols.sum_columns()
    gram_cols.gather_x()
    loop_factor(gram_cols.result(), total_cols, work)
    inverse_cols = inverse_of(work)
    for b in range(columns_ref.shape[0]):
        basis_ref[:, b * LANE : (b + 1) * LANE] = apply_inverse(inverse_cols, columns_ref[b]).astype(
            bf16
        )

    spread = Spread(n_row, row, col, chunks, r, "two_")
    sums = [RowSums(n_col, row, col, c, r, "two_") for c in range(chunks)]
    spread.start(basis_ref)
    for c in range(chunks):
        spread.finish(c)
        sums[c].sketch(spread.got[c], splits, info)
        sums[c].start()
        sums[c].pair_up()
    for c in range(chunks):
        held_ref[:, c * rows : (c + 1) * rows] = sums[c].total()
    gram_two = GramSum(sizes, row, col, r, "gram_two_")
    gram_two.scatter_x(pack_gram(gram_of(held_ref[0]) + gram_of(held_ref[1])))
    gram_two.sum_z()
    gram_two.sum_columns()
    gram_two.gather_x()
    gram_ref[...] = gram_two.result()


def whole_scratch(sizes, chunks, capacity, width, per_owner, block):
    n_row, n_col, nx = sizes
    named = {
        "wanted": pltpu.VMEM((n_row, 1, LANE), jnp.int32),
        "id_send": pltpu.SemaphoreType.DMA((n_row,)),
        "id_recv": pltpu.SemaphoreType.DMA((n_row,)),
        "high": pltpu.VMEM((capacity, block, block), bf16),
        "middle": pltpu.VMEM((capacity, block, block), bf16),
        "low": pltpu.VMEM((capacity, block, block), bf16),
        "columns": pltpu.VMEM((per_owner, width, LANE), f32),
        "held": pltpu.VMEM((2, width, LANE), f32),
        "work": pltpu.VMEM((width, LANE), f32),
    }
    for tag in ("gram_one_", "gram_cols_", "gram_two_"):
        named.update(gram_scratch(sizes, tag))
    named.update(spread_scratch(n_row, chunks, width, "one_"))
    named.update(spread_scratch(n_row, chunks, width, "two_"))
    named.update(row_scratch(n_col, capacity, chunks, width, "one_", True))
    named.update(row_scratch(n_col, capacity, chunks, width, "two_", False))
    named.update(column_scratch(n_row, capacity, chunks, width))
    return named


def factor(gram_ref, count):
    packed = gram_ref[...].reshape(32, LANE)
    lane = lax.broadcasted_iota(jnp.int32, (8, LANE), 1)
    sub = lax.broadcasted_iota(jnp.int32, (8, LANE), 0)
    turned = pltpu.roll(packed, 64, 1)
    groups = []
    for g in range(8):
        source = packed if g < 4 else turned
        h = g % 4
        left = source[h * 8 : (h + 1) * 8] * (1.0 / count)
        ident = jnp.where(lane - 64 == sub + g * 8, 1.0, 0.0).astype(f32)
        groups.append(jnp.where(lane < 64, left, ident))
    pivots = []
    for kb in range(8):
        below = range(kb, 8)
        cols = [
            {g: jnp.broadcast_to(groups[g][:, 8 * kb + i : 8 * kb + i + 1], (8, LANE)) for g in below}
            for i in range(8)
        ]
        lines = [jnp.broadcast_to(groups[kb][i : i + 1, :], (8, LANE)) for i in range(8)]
        scaled = []
        diagonal = jnp.ones((8, LANE), f32)
        for i in range(8):
            pivot = jnp.broadcast_to(cols[i][kb][i : i + 1, :], (8, LANE))
            diagonal = jnp.where(sub == i, pivot, diagonal)
            inverse = 1.0 / pivot
            scaled.append(lines[i] * inverse)
            for j in range(i + 1, 8):
                ratio = jnp.broadcast_to(cols[i][kb][j : j + 1, :], (8, LANE)) * inverse
                lines[j] = lines[j] - ratio * lines[i]
                for g in below:
                    cols[j][g] = cols[j][g] - cols[i][g] * ratio
        block = lines[0]
        for i in range(1, 8):
            block = jnp.where(sub == i, lines[i], block)
        groups[kb] = block
        pivots.append(diagonal)
        for g in range(kb + 1, 8):
            for i in range(8):
                groups[g] = groups[g] - cols[i][g] * scaled[i]
    return [groups[g] / jnp.sqrt(pivots[g]) for g in range(8)]


def split_factor(groups):
    both = jnp.concatenate(groups, axis=0)
    lane = lax.broadcasted_iota(jnp.int32, both.shape, 1)
    sub = lax.broadcasted_iota(jnp.int32, both.shape, 0)
    upper = jnp.where((lane < 64) & (lane >= sub), both, 0.0)
    inverse = jnp.where(lane < 64, pltpu.roll(both, 64, 1), 0.0)
    return upper, inverse


def apply_inverse(inverse, block):
    return nn(inverse, jnp.concatenate([block, jnp.zeros_like(block)], axis=0))


def final_kernel(count, gram_ref, held_ref, basis_ref, q_ref, w_ref, r_ref):
    upper, inverse = split_factor(factor(gram_ref, count))
    r_ref[...] = upper[:, :64]
    w_ref[...] = basis_ref[...]
    for b in range(held_ref.shape[0]):
        q_ref[:, b * LANE : (b + 1) * LANE] = apply_inverse(inverse, held_ref[b])


def call(body, outs, ins, scratch=(), smem=0, collective=None):
    vmem = pl.BlockSpec(memory_space=pltpu.VMEM)
    return pl.pallas_call(
        body,
        out_shape=[jax.ShapeDtypeStruct(shape, kind) for shape, kind in outs],
        in_specs=[pl.BlockSpec(memory_space=pltpu.SMEM)] * smem + [vmem] * (len(ins) - smem),
        out_specs=[vmem] * len(outs),
        scratch_shapes=list(scratch),
        compiler_params=pltpu.CompilerParams(
            collective_id=collective,
            has_side_effects=collective is not None,
            vmem_limit_bytes=24 * 1024 * 1024,
        ),
    )(*ins)


def shards(n_row, n_col, nx, tiles, coords, counts, probes):
    sizes = (n_row, n_col, nx)
    capacity, block = tiles.shape[0], tiles.shape[1]
    width, share = probes.shape[0], probes.shape[2]
    per_owner = share // block
    group_blocks = 2 * n_col
    total_rows = group_blocks * n_row * block
    total_cols = share * n_row * n_col
    order = jnp.arange(capacity, dtype=jnp.int32)
    live = order < counts[0]
    place = coords[:, 0] % group_blocks
    col_local = coords[:, 1] % (per_owner * n_row)
    owner = col_local // per_owner
    within = col_local % per_owner

    def latest(keys, wanted, allowed):
        match = (keys[:, None] == wanted[None, :]) & live[:, None] & allowed
        found = jnp.max(jnp.where(match, order[:, None], -1), axis=0)
        return jnp.where(found < 0, capacity, found)

    rows_wanted = jnp.arange(group_blocks, dtype=jnp.int32)
    owners = jnp.arange(n_row, dtype=jnp.int32)
    before = latest(place, place, order[:, None] < order[None, :])
    info = jnp.concatenate(
        [owner, place, before, latest(place, rows_wanted, True), latest(owner, owners, True)]
    ).astype(jnp.int32)
    match = (owner[:, None] == owners[None, :]) & live[:, None]
    ids = jnp.sum(jnp.where(match, within[:, None] + 1, 0), axis=0)
    ids = jnp.broadcast_to(ids[:, None, None], (n_row, 1, LANE)).astype(jnp.int32)

    scratch = whole_scratch(sizes, CHUNKS, capacity, width, per_owner, block)
    held, gram, basis = call(
        functools.partial(whole_kernel, sizes, CHUNKS, (total_rows, total_cols), list(scratch)),
        [((2, width, LANE), f32), ((32, LANE), f32), ((width, share), bf16)],
        (info, tiles, probes.reshape(width, share), ids),
        scratch.values(),
        smem=1,
        collective=0,
    )
    q_basis, w_basis, r_factor = call(
        functools.partial(final_kernel, total_rows),
        [((width, 2 * LANE), f32), ((width, share), bf16), ((width, width), f32)],
        (gram, held, basis),
    )
    return (q_basis, w_basis.reshape(width, 1, share), r_factor)


def solution(mesh):
    n_row, n_col = mesh.shape["row"], mesh.shape["col"]
    nx = 4 if n_row >= 16 else 2
    in_specs = (
        P(("row", "col"), None, None),
        P(("row", "col"), None),
        P(("row", "col")),
        P(None, "col", "row"),
    )
    out_specs = (P(None, ("row", "col")), P(None, "col", "row"), P())
    return jax.shard_map(
        functools.partial(shards, n_row, n_col, nx),
        mesh=mesh,
        in_specs=in_specs,
        out_specs=out_specs,
        check_vma=False,
    )
```

```python
import functools

import jax
import jax.numpy as jnp
from jax import lax
from jax.experimental import pallas as pl
from jax.experimental.pallas import tpu as pltpu
from jax.sharding import PartitionSpec as P

MESH = pl.DeviceIdType.MESH
highest = lax.Precision.HIGHEST
f32 = jnp.float32
bf16 = jnp.bfloat16
LANE = 128
CORES = 2
CHUNKS = 2


def nn(left, right):
    return lax.dot_general(
        left, right, (((1,), (0,)), ((), ())), precision=highest, preferred_element_type=f32
    )


def nt(left, right):
    return lax.dot_general(
        left, right, (((1,), (1,)), ((), ())), precision=highest, preferred_element_type=f32
    )


def remote(src, dst, send, recv, device):
    return pltpu.make_async_remote_copy(
        src_ref=src,
        dst_ref=dst,
        send_sem=send,
        recv_sem=recv,
        device_id=device,
        device_id_type=MESH,
    )


def loop(lower, upper, body):
    def step(i, carry):
        body(i)
        return carry

    lax.fori_loop(lower, upper, step, 0)


def offset(k, n):
    step = (k + 1) // 2
    return n // 2 + step * (2 * lax.rem(k, 2) - 1)


def greet(n_row, n_col, row, col, with_row, with_col):
    barrier = pltpu.get_barrier_semaphore()
    count = 0
    if with_row:
        loop(
            1,
            n_row,
            lambda d: pl.semaphore_signal(
                barrier, inc=1, device_id=(lax.rem(row + d, n_row), col), device_id_type=MESH
            ),
        )
        count += n_row - 1
    if with_col:
        loop(
            1,
            n_col,
            lambda d: pl.semaphore_signal(
                barrier, inc=1, device_id=(row, lax.rem(col + d, n_col)), device_id_type=MESH
            ),
        )
        count += n_col - 1
    pl.semaphore_wait(barrier, count)


class Exchange:
    def __init__(self, n, me, source, dst, send, recv, device, each=False):
        self.n, self.me, self.source, self.dst = n, me, source, dst
        self.send, self.recv, self.device, self.each = send, recv, device, each

    def copy(self, peer, slot):
        send = self.send.at[peer] if self.each else self.send
        recv = self.recv.at[slot] if self.each else self.recv
        return remote(self.source(peer), self.dst.at[slot], send, recv, self.device(peer))

    def copy_to(self, peer):
        return self.copy(peer, self.me)

    def copy_from(self, peer):
        return self.copy(peer, peer)

    def start(self):
        loop(
            0, self.n - 1, lambda k: self.copy_to(lax.rem(self.me + offset(k, self.n), self.n)).start()
        )

    def wait(self):
        if self.n == 1:
            return
        everything = self.dst.at[pl.ds(0, self.n - 1)]
        device = self.device(lax.rem(self.me + 1, self.n))
        remote(everything, everything, self.send, self.recv, device).wait()


def sum_slots(ref, n):
    total = ref[0]
    for s in range(1, n):
        total = total + ref[s]
    return total


def gram_of(block):
    return nt(block, jnp.concatenate([block, jnp.zeros_like(block)], axis=0))


def pack_gram(gram):
    half = gram.shape[0] // 2
    return gram[:half] + pltpu.roll(gram[half:], 64, 1)


class GramSum:
    def __init__(self, sizes, row, col, r, tag):
        n_row, n_col, nx = sizes
        nz = n_row // nx
        z, x = row // nx, lax.rem(row, nx)
        self.nx, self.nz, self.nc, self.x, self.z, self.col = nx, nz, n_col, x, z, col
        get = lambda name: r[tag + name]
        self.part, self.gx, self.s1, self.gz = get("part"), get("gx"), get("s1"), get("gz")
        self.s2, self.gc, self.out = get("s2"), get("gc"), get("out")
        along_x = lambda p: (z * nx + p, col)
        along_z = lambda p: (p * nx + x, col)
        along_c = lambda p: (row, p)
        part, s1, s2, out = self.part, self.s1, self.s2, self.out
        self.first = Exchange(
            nx, x, lambda p: part.at[p], self.gx, get("x_send"), get("x_recv"), along_x
        )
        self.second = Exchange(nz, z, lambda p: s1, self.gz, get("z_send"), get("z_recv"), along_z)
        self.third = Exchange(
            n_col, col, lambda p: s2, self.gc, get("c_send"), get("c_recv"), along_c
        )
        self.last = Exchange(
            nx, x, lambda p: out.at[x], out, get("o_send"), get("o_recv"), along_x
        )

    def scatter_x(self, packed):
        depth = packed.shape[0] // self.nx
        for j in range(self.nx):
            self.part[j] = packed[j * depth : (j + 1) * depth]
        self.first.start()
        self.gx[self.x] = self.part[self.x]

    def sum_z(self):
        self.first.wait()
        self.s1[...] = sum_slots(self.gx, self.nx)
        self.second.start()
        self.gz[self.z] = self.s1[...]

    def sum_columns(self):
        self.second.wait()
        self.s2[...] = sum_slots(self.gz, self.nz)
        self.third.start()
        self.gc[self.col] = self.s2[...]

    def gather_x(self):
        self.third.wait()
        self.out[self.x] = sum_slots(self.gc, self.nc)
        self.last.start()

    def result(self):
        self.last.wait()
        return self.out[...].reshape(32, LANE)


def gram_scratch(sizes, tag):
    n_row, n_col, nx = sizes
    depth = 32 // nx
    nz = n_row // nx
    dma = pltpu.SemaphoreType.DMA
    named = {
        "part": pltpu.VMEM((nx, depth, LANE), f32),
        "gx": pltpu.VMEM((nx, depth, LANE), f32),
        "s1": pltpu.VMEM((depth, LANE), f32),
        "gz": pltpu.VMEM((nz, depth, LANE), f32),
        "s2": pltpu.VMEM((depth, LANE), f32),
        "gc": pltpu.VMEM((n_col, depth, LANE), f32),
        "out": pltpu.VMEM((nx, depth, LANE), f32),
        "x_send": dma,
        "x_recv": dma,
        "z_send": dma,
        "z_recv": dma,
        "c_send": dma,
        "c_recv": dma,
        "o_send": dma,
        "o_recv": dma,
    }
    return {tag + name: shape for name, shape in named.items()}


def pick(own, wanted):
    wanted = jnp.broadcast_to(wanted, (own.shape[0], LANE))
    total = jnp.zeros((own.shape[0], LANE), f32)
    for b in range(own.shape[1] // LANE):
        total = jnp.where(wanted == b + 1, own[:, b * LANE : (b + 1) * LANE].astype(f32), total)
    return total.astype(bf16)


class Spread:
    def __init__(self, n_row, row, col, chunks, r, tag):
        self.n_row, self.row, self.chunks = n_row, row, chunks
        self.wanted = r["wanted"]
        self.outgoing = [r[tag + "outgoing%d" % c] for c in range(chunks)]
        self.got = [r[tag + "got%d" % c] for c in range(chunks)]
        self.moves = [
            Exchange(
                n_row,
                row,
                functools.partial(lambda ref, p: ref.at[p], self.outgoing[c]),
                self.got[c],
                r[tag + "send%d" % c],
                r[tag + "recv%d" % c],
                lambda p: (p, col),
                c + 1 < chunks,
            )
            for c in range(chunks)
        ]

    def store(self, refs, place, block):
        rows = block.shape[0] // self.chunks
        for c in range(self.chunks):
            refs[c][place] = block[c * rows : (c + 1) * rows]

    def start(self, own_ref, ready=None):
        def serve(k):
            peer = lax.rem(self.row - offset(k, self.n_row) + self.n_row, self.n_row)
            if ready is not None:
                ready(peer)
            self.store(self.outgoing, peer, pick(own_ref[...], self.wanted[peer]))
            self.moves[0].copy_to(peer).start()

        loop(0, self.n_row - 1, serve)
        self.store(self.got, self.row, pick(own_ref[...], self.wanted[self.row]))

    def finish(self, c):
        if c + 1 == self.chunks:
            self.moves[c].wait()
            return

        def step(k):
            peer = lax.rem(self.row - offset(k, self.n_row) + self.n_row, self.n_row)
            self.moves[c].copy_from(peer).wait()
            self.moves[c + 1].copy_to(peer).start()

        loop(0, self.n_row - 1, step)


def spread_scratch(n_row, chunks, width, tag):
    rows = width // chunks
    named = {}
    for c in range(chunks):
        named[tag + "outgoing%d" % c] = pltpu.VMEM((n_row, rows, LANE), bf16)
        named[tag + "got%d" % c] = pltpu.VMEM((n_row, rows, LANE), bf16)
        for name in ("send%d", "recv%d"):
            each = pltpu.SemaphoreType.DMA((n_row,))
            named[tag + name % c] = each if c + 1 < chunks else pltpu.SemaphoreType.DMA
    return named


class RowSums:
    def __init__(self, n_col, row, col, c, r, tag):
        self.ny = ny = n_col // CORES
        self.n_col = n_col
        self.y, self.core = col // CORES, lax.rem(col, CORES)
        self.row, self.col = row, col
        self.other = col + 1 - 2 * self.core
        get = lambda name: r[tag + name + "%d" % c]
        self.terms, self.part, self.near = get("contrib"), get("rows"), get("near")
        self.near_send, self.near_recv = get("near_send"), get("near_recv")
        self.summed, self.far = get("summed"), get("far")
        self.shares = Exchange(
            ny,
            self.y,
            lambda p: self.summed.at[p],
            self.far,
            get("far_send"),
            get("far_recv"),
            self.same_core,
        )
        if tag + "group%d" % c in r:
            self.group = get("group")
            self.all_send, self.all_recv = get("all_send"), get("all_recv")
            self.pass_send, self.pass_recv = get("pass_send"), get("pass_recv")

    def same_core(self, p):
        return (self.row, p * CORES + self.core)

    def near_copy(self, t):
        return remote(
            self.part.at[t * CORES + (1 - self.core)],
            self.near.at[t],
            self.near_send.at[t],
            self.near_recv.at[t],
            (self.row, self.other),
        )

    def peer(self, k):
        return lax.rem(self.y + offset(k, self.ny), self.ny)

    def sketch(self, got, splits, info):
        capacity = splits[0].shape[0]
        dims = (((1,), (1,)), ((), ()))
        for t in range(capacity):
            block = got[info["owner"](t)]
            total = lax.dot_general(block, splits[2][t], dims, preferred_element_type=f32)
            total += lax.dot_general(block, splits[1][t], dims, preferred_element_type=f32)
            total += lax.dot_general(block, splits[0][t], dims, preferred_element_type=f32)
            self.terms[t] = total
        self.terms[capacity] = jnp.zeros(self.terms.shape[1:], f32)

        def chain(t):
            self.terms[t] = self.terms[t] + self.terms[info["before"](t)]

        loop(0, capacity, chain)

        def place(p):
            for j in range(2):
                self.part[p, j] = self.terms[info["last"](2 * p + j)]

        loop(0, self.n_col, place)

    def start(self):
        loop(0, self.ny - 1, lambda k: self.near_copy(self.peer(k)).start())
        self.near_copy(self.y).start()

    def pair_up(self):
        def step(k):
            peer = self.peer(k)
            self.near_copy(peer).wait()
            self.summed[peer] = self.part[peer * CORES + self.core] + self.near[peer]
            self.shares.copy_to(peer).start()

        loop(0, self.ny - 1, step)
        self.near_copy(self.y).wait()
        self.far[self.y] = self.part[self.y * CORES + self.core] + self.near[self.y]

    def total(self):
        self.shares.wait()
        return sum_slots(self.far, self.ny)

    def pass_copy(self, slot, peer):
        return remote(
            self.group.at[slot],
            self.group.at[slot],
            self.pass_send.at[peer],
            self.pass_recv.at[peer],
            (self.row, self.other),
        )

    def gather(self, total):
        self.group[self.col] = total
        mine = self.group.at[self.col]

        def send(k):
            peer = self.peer(k)
            remote(
                mine, mine, self.all_send.at[peer], self.all_recv.at[self.y], self.same_core(peer)
            ).start()

        loop(0, self.ny - 1, send)
        self.pass_copy(self.col, self.y).start()

    def gathered(self):
        def relay(k):
            peer = lax.rem(self.y - offset(k, self.ny) + self.ny, self.ny)
            slot = peer * CORES + self.core
            remote(
                self.group.at[self.col],
                self.group.at[slot],
                self.all_send.at[peer],
                self.all_recv.at[peer],
                self.same_core(peer),
            ).wait()
            self.pass_copy(slot, peer).start()

        loop(0, self.ny - 1, relay)
        loop(0, self.ny, lambda p: self.pass_copy(p * CORES + (1 - self.core), p).wait())


def row_scratch(n_col, capacity, chunks, width, tag, gather):
    ny = n_col // CORES
    rows = width // chunks
    dma = pltpu.SemaphoreType.DMA
    named = {}
    for c in range(chunks):
        some = {
            "contrib": pltpu.VMEM((capacity + 1, rows, LANE), f32),
            "rows": pltpu.VMEM((n_col, 2, rows, LANE), f32),
            "near": pltpu.VMEM((ny, 2, rows, LANE), f32),
            "summed": pltpu.VMEM((ny, 2, rows, LANE), f32),
            "far": pltpu.VMEM((ny, 2, rows, LANE), f32),
        }
        some["far_send"] = some["far_recv"] = dma
        sems = ["near_send", "near_recv"]
        if gather:
            some["group"] = pltpu.VMEM((n_col, 2, rows, LANE), f32)
            sems += ["all_send", "all_recv", "pass_send", "pass_recv"]
        for name in sems:
            some[name] = dma((ny,))
        for name, shape in some.items():
            named[tag + name + "%d" % c] = shape
    return named


def three(value):
    high = value.astype(bf16)
    rest = value - high.astype(f32)
    middle = rest.astype(bf16)
    return high, middle, (rest - middle.astype(f32)).astype(bf16)


class ColumnSums:
    def __init__(self, n_row, row, col, c, r):
        self.n_row, self.row = n_row, row
        self.terms, self.outgoing, self.arrived = (
            r["terms%d" % c],
            r["leaving%d" % c],
            r["arrived%d" % c],
        )
        self.wanted = r["wanted"]
        self.moved = Exchange(
            n_row,
            row,
            lambda p: self.outgoing.at[p],
            self.arrived,
            r["leaving_send%d" % c],
            r["leaving_recv%d" % c],
            lambda p: (p, col),
        )

    def start(self, group, splits, info):
        capacity = splits[0].shape[0]
        rows = self.terms.shape[1]

        def dot(left, right):
            return lax.dot_general(
                left, right, (((1,), (0,)), ((), ())), preferred_element_type=f32
            )

        for t in range(capacity):
            place = info["place"](t)
            source = group[place // 2, lax.rem(place, 2)]
            high, middle, low = three(source)
            by_high = dot(jnp.concatenate([high, middle, low], axis=0), splits[0][t])
            by_middle = dot(jnp.concatenate([high, middle], axis=0), splits[1][t])
            by_low = dot(high, splits[2][t])
            small = by_high[2 * rows :] + by_middle[rows:] + by_low
            self.terms[t] = by_high[:rows] + (by_high[rows : 2 * rows] + by_middle[:rows] + small)
        self.terms[capacity] = jnp.zeros(self.terms.shape[1:], f32)

        def serve(k):
            peer = lax.rem(self.row + offset(k, self.n_row), self.n_row)
            self.outgoing[peer] = self.terms[info["slot"](peer)]
            self.moved.copy_to(peer).start()

        loop(0, self.n_row - 1, serve)
        self.arrived[self.row] = self.terms[info["slot"](self.row)]

    def finish(self, columns_ref, first):
        self.moved.wait()
        rows = self.arrived.shape[1]

        def column(b):
            def add(q, total):
                for j in range(8):
                    s = 8 * q + j
                    hit = jnp.broadcast_to(self.wanted[s], (rows, LANE)) == b + 1
                    total = total + jnp.where(hit, self.arrived[s], 0.0)
                return total

            columns_ref[b, first : first + rows] = lax.fori_loop(
                0, self.n_row // 8, add, jnp.zeros((rows, LANE), f32)
            )

        loop(0, columns_ref.shape[0], column)


def column_scratch(n_row, capacity, chunks, width):
    rows = width // chunks
    named = {}
    for c in range(chunks):
        named["terms%d" % c] = pltpu.VMEM((capacity + 1, rows, LANE), f32)
        named["leaving%d" % c] = pltpu.VMEM((n_row, rows, LANE), f32)
        named["arrived%d" % c] = pltpu.VMEM((n_row, rows, LANE), f32)
        named["leaving_send%d" % c] = pltpu.SemaphoreType.DMA
        named["leaving_recv%d" % c] = pltpu.SemaphoreType.DMA
    return named


def loop_factor(packed, count, work):
    lane = lax.broadcasted_iota(jnp.int32, (64, LANE), 1)
    line = lax.broadcasted_iota(jnp.int32, (64, LANE), 0)
    sub = lax.broadcasted_iota(jnp.int32, (8, LANE), 0)
    gram = jnp.concatenate([packed, pltpu.roll(packed, 64, 1)], axis=0) * (1.0 / count)
    work[...] = jnp.where(lane < 64, gram, jnp.where(lane - 64 == line, 1.0, 0.0))

    def eliminate(kb):
        base = pl.multiple_of(kb * 8, 8)
        shift = lax.rem(LANE - base, LANE)
        block = work[pl.ds(base, 8), :]
        whole = work[...]
        near = pltpu.roll(block, shift, 1)
        far = pltpu.roll(whole, shift, 1)
        heads = [jnp.broadcast_to(near[:, i : i + 1], (8, LANE)) for i in range(8)]
        cols = [jnp.broadcast_to(far[:, i : i + 1], (64, LANE)) for i in range(8)]
        lines = [jnp.broadcast_to(block[i : i + 1, :], (8, LANE)) for i in range(8)]
        diagonal = jnp.ones((8, LANE), f32)
        total = jnp.zeros((64, LANE), f32)
        final = lines[0]
        for i in range(8):
            pivot = jnp.broadcast_to(heads[i][i : i + 1, :], (8, LANE))
            diagonal = jnp.where(sub == i, pivot, diagonal)
            final = jnp.where(sub == i, lines[i], final)
            inverse = 1.0 / pivot
            scaled = lines[i] * inverse
            total = total + cols[i] * jnp.broadcast_to(scaled[:1], (64, LANE))
            for j in range(i + 1, 8):
                ratio = jnp.broadcast_to(heads[i][j : j + 1, :], (8, LANE)) * inverse
                lines[j] = lines[j] - ratio * lines[i]
                heads[j] = heads[j] - heads[i] * ratio
                cols[j] = cols[j] - cols[i] * jnp.broadcast_to(ratio[:1], (64, LANE))
        work[...] = whole - jnp.where(line >= base + 8, total, 0.0)
        work[pl.ds(base, 8), :] = final / jnp.sqrt(diagonal)

    loop(0, 8, eliminate)


def inverse_of(work):
    both = work[...]
    lane = lax.broadcasted_iota(jnp.int32, both.shape, 1)
    return jnp.where(lane < 64, pltpu.roll(both, 64, 1), 0.0)


def whole_kernel(sizes, chunks, totals, names, info_ref, tiles_ref, own_ref, ids_ref, *refs):
    n_row, n_col, nx = sizes
    total_rows, total_cols = totals
    held_ref, gram_ref, basis_ref = refs[:3]
    r = dict(zip(names, refs[3:]))
    row, col = lax.axis_index("row"), lax.axis_index("col")
    capacity = tiles_ref.shape[0]
    starts = {"owner": 0, "place": capacity, "before": 2 * capacity, "last": 3 * capacity}
    starts["slot"] = 3 * capacity + 2 * n_col
    info = {
        name: functools.partial(lambda first, i: info_ref[first + i], first)
        for name, first in starts.items()
    }
    splits = [r["high"], r["middle"], r["low"]]
    wanted = r["wanted"]
    width = own_ref.shape[0]
    rows = width // chunks
    columns_ref, work, held = r["columns"], r["work"], r["held"]

    greet(n_row, n_col, row, col, True, True)
    ids = Exchange(
        n_row,
        row,
        lambda p: ids_ref.at[p],
        wanted,
        r["id_send"],
        r["id_recv"],
        lambda p: (p, col),
        True,
    )
    ids.start()
    wanted[row] = ids_ref[row]

    def split(t):
        for ref, piece in zip(splits, three(tiles_ref[t])):
            ref[t] = piece

    loop(0, capacity, split)

    spread = Spread(n_row, row, col, chunks, r, "one_")
    sums = [RowSums(n_col, row, col, c, r, "one_") for c in range(chunks)]
    spread.start(own_ref, lambda peer: ids.copy_from(peer).wait())
    gram_one = GramSum(sizes, row, col, r, "gram_one_")
    moves = [ColumnSums(n_row, row, col, c, r) for c in range(chunks)]

    def gather(c):
        total = sums[c].total()
        sums[c].gather(total)
        held[:, c * rows : (c + 1) * rows] = total

    def send_terms(c):
        sums[c].gathered()
        moves[c].start(sums[c].group, splits, info)

    for c in range(chunks):
        spread.finish(c)
        sums[c].sketch(spread.got[c], splits, info)
        sums[c].start()
        if c >= 1:
            gather(c - 1)
        sums[c].pair_up()
        if c >= 1:
            send_terms(c - 1)
    last = chunks - 1
    gather(last)
    gram_one.scatter_x(pack_gram(gram_of(held[0]) + gram_of(held[1])))
    gram_one.sum_z()
    gram_one.sum_columns()
    sums[last].gathered()
    gram_one.gather_x()
    moves[last].start(sums[last].group, splits, info)
    loop_factor(gram_one.result(), total_rows, work)
    inverse_one = inverse_of(work)
    for c in range(chunks):
        moves[c].finish(columns_ref, c * rows)

    total = jnp.zeros((width, LANE), f32)
    for b in range(columns_ref.shape[0]):
        block = apply_inverse(inverse_one, columns_ref[b])
        columns_ref[b] = block
        total = total + gram_of(block)
    packed = pack_gram(total)
    gram_cols = GramSum(sizes, row, col, r, "gram_cols_")
    gram_cols.scatter_x(packed)
    gram_cols.sum_z()
    gram_cols.sum_columns()
    gram_cols.gather_x()
    gram_cols.last.wait()
    unused, inverse_cols = split_factor(factor(gram_cols.out, total_cols))
    for b in range(columns_ref.shape[0]):
        basis_ref[:, b * LANE : (b + 1) * LANE] = apply_inverse(inverse_cols, columns_ref[b]).astype(
            bf16
        )

    spread = Spread(n_row, row, col, chunks, r, "two_")
    sums = [RowSums(n_col, row, col, c, r, "two_") for c in range(chunks)]
    spread.start(basis_ref)
    for c in range(chunks):
        spread.finish(c)
        sums[c].sketch(spread.got[c], splits, info)
        sums[c].start()
        sums[c].pair_up()
    for c in range(chunks):
        held_ref[:, c * rows : (c + 1) * rows] = sums[c].total()
    gram_two = GramSum(sizes, row, col, r, "gram_two_")
    gram_two.scatter_x(pack_gram(gram_of(held_ref[0]) + gram_of(held_ref[1])))
    gram_two.sum_z()
    gram_two.sum_columns()
    gram_two.gather_x()
    gram_ref[...] = gram_two.result()


def whole_scratch(sizes, chunks, capacity, width, per_owner, block):
    n_row, n_col, nx = sizes
    named = {
        "wanted": pltpu.VMEM((n_row, 1, LANE), jnp.int32),
        "id_send": pltpu.SemaphoreType.DMA((n_row,)),
        "id_recv": pltpu.SemaphoreType.DMA((n_row,)),
        "high": pltpu.VMEM((capacity, block, block), bf16),
        "middle": pltpu.VMEM((capacity, block, block), bf16),
        "low": pltpu.VMEM((capacity, block, block), bf16),
        "columns": pltpu.VMEM((per_owner, width, LANE), f32),
        "held": pltpu.VMEM((2, width, LANE), f32),
        "work": pltpu.VMEM((width, LANE), f32),
    }
    for tag in ("gram_one_", "gram_cols_", "gram_two_"):
        named.update(gram_scratch(sizes, tag))
    named.update(spread_scratch(n_row, chunks, width, "one_"))
    named.update(spread_scratch(n_row, chunks, width, "two_"))
    named.update(row_scratch(n_col, capacity, chunks, width, "one_", True))
    named.update(row_scratch(n_col, capacity, chunks, width, "two_", False))
    named.update(column_scratch(n_row, capacity, chunks, width))
    return named


def factor(gram_ref, count):
    packed = gram_ref[...].reshape(32, LANE)
    lane = lax.broadcasted_iota(jnp.int32, (8, LANE), 1)
    sub = lax.broadcasted_iota(jnp.int32, (8, LANE), 0)
    turned = pltpu.roll(packed, 64, 1)
    groups = []
    for g in range(8):
        source = packed if g < 4 else turned
        h = g % 4
        left = source[h * 8 : (h + 1) * 8] * (1.0 / count)
        ident = jnp.where(lane - 64 == sub + g * 8, 1.0, 0.0).astype(f32)
        groups.append(jnp.where(lane < 64, left, ident))
    pivots = []
    for kb in range(8):
        below = range(kb, 8)
        cols = [
            {g: jnp.broadcast_to(groups[g][:, 8 * kb + i : 8 * kb + i + 1], (8, LANE)) for g in below}
            for i in range(8)
        ]
        lines = [jnp.broadcast_to(groups[kb][i : i + 1, :], (8, LANE)) for i in range(8)]
        scaled = []
        diagonal = jnp.ones((8, LANE), f32)
        for i in range(8):
            pivot = jnp.broadcast_to(cols[i][kb][i : i + 1, :], (8, LANE))
            diagonal = jnp.where(sub == i, pivot, diagonal)
            inverse = 1.0 / pivot
            scaled.append(lines[i] * inverse)
            for j in range(i + 1, 8):
                ratio = jnp.broadcast_to(cols[i][kb][j : j + 1, :], (8, LANE)) * inverse
                lines[j] = lines[j] - ratio * lines[i]
                for g in below:
                    cols[j][g] = cols[j][g] - cols[i][g] * ratio
        block = lines[0]
        for i in range(1, 8):
            block = jnp.where(sub == i, lines[i], block)
        groups[kb] = block
        pivots.append(diagonal)
        for g in range(kb + 1, 8):
            for i in range(8):
                groups[g] = groups[g] - cols[i][g] * scaled[i]
    return [groups[g] / jnp.sqrt(pivots[g]) for g in range(8)]


def split_factor(groups):
    both = jnp.concatenate(groups, axis=0)
    lane = lax.broadcasted_iota(jnp.int32, both.shape, 1)
    sub = lax.broadcasted_iota(jnp.int32, both.shape, 0)
    upper = jnp.where((lane < 64) & (lane >= sub), both, 0.0)
    inverse = jnp.where(lane < 64, pltpu.roll(both, 64, 1), 0.0)
    return upper, inverse


def apply_inverse(inverse, block):
    return nn(inverse, jnp.concatenate([block, jnp.zeros_like(block)], axis=0))


def final_kernel(count, gram_ref, held_ref, basis_ref, q_ref, w_ref, r_ref):
    upper, inverse = split_factor(factor(gram_ref, count))
    r_ref[...] = upper[:, :64]
    w_ref[...] = basis_ref[...]
    for b in range(held_ref.shape[0]):
        q_ref[:, b * LANE : (b + 1) * LANE] = apply_inverse(inverse, held_ref[b])


def call(body, outs, ins, scratch=(), smem=0, collective=None):
    vmem = pl.BlockSpec(memory_space=pltpu.VMEM)
    return pl.pallas_call(
        body,
        out_shape=[jax.ShapeDtypeStruct(shape, kind) for shape, kind in outs],
        in_specs=[pl.BlockSpec(memory_space=pltpu.SMEM)] * smem + [vmem] * (len(ins) - smem),
        out_specs=[vmem] * len(outs),
        scratch_shapes=list(scratch),
        compiler_params=pltpu.CompilerParams(
            collective_id=collective,
            has_side_effects=collective is not None,
            vmem_limit_bytes=24 * 1024 * 1024,
        ),
    )(*ins)


def shards(n_row, n_col, nx, tiles, coords, counts, probes):
    sizes = (n_row, n_col, nx)
    capacity, block = tiles.shape[0], tiles.shape[1]
    width, share = probes.shape[0], probes.shape[2]
    per_owner = share // block
    group_blocks = 2 * n_col
    total_rows = group_blocks * n_row * block
    total_cols = share * n_row * n_col
    order = jnp.arange(capacity, dtype=jnp.int32)
    live = order < counts[0]
    place = coords[:, 0] % group_blocks
    col_local = coords[:, 1] % (per_owner * n_row)
    owner = col_local // per_owner
    within = col_local % per_owner

    def latest(keys, wanted, allowed):
        match = (keys[:, None] == wanted[None, :]) & live[:, None] & allowed
        found = jnp.max(jnp.where(match, order[:, None], -1), axis=0)
        return jnp.where(found < 0, capacity, found)

    rows_wanted = jnp.arange(group_blocks, dtype=jnp.int32)
    owners = jnp.arange(n_row, dtype=jnp.int32)
    before = latest(place, place, order[:, None] < order[None, :])
    info = jnp.concatenate(
        [owner, place, before, latest(place, rows_wanted, True), latest(owner, owners, True)]
    ).astype(jnp.int32)
    match = (owner[:, None] == owners[None, :]) & live[:, None]
    ids = jnp.sum(jnp.where(match, within[:, None] + 1, 0), axis=0)
    ids = jnp.broadcast_to(ids[:, None, None], (n_row, 1, LANE)).astype(jnp.int32)

    scratch = whole_scratch(sizes, CHUNKS, capacity, width, per_owner, block)
    held, gram, basis = call(
        functools.partial(whole_kernel, sizes, CHUNKS, (total_rows, total_cols), list(scratch)),
        [((2, width, LANE), f32), ((32, LANE), f32), ((width, share), bf16)],
        (info, tiles, probes.reshape(width, share), ids),
        scratch.values(),
        smem=1,
        collective=0,
    )
    q_basis, w_basis, r_factor = call(
        functools.partial(final_kernel, total_rows),
        [((width, 2 * LANE), f32), ((width, share), bf16), ((width, width), f32)],
        (gram, held, basis),
    )
    return (q_basis, w_basis.reshape(width, 1, share), r_factor)


def solution(mesh):
    n_row, n_col = mesh.shape["row"], mesh.shape["col"]
    nx = 4 if n_row >= 16 else 2
    in_specs = (
        P(("row", "col"), None, None),
        P(("row", "col"), None),
        P(("row", "col")),
        P(None, "col", "row"),
    )
    out_specs = (P(None, ("row", "col")), P(None, "col", "row"), P())
    return jax.shard_map(
        functools.partial(shards, n_row, n_col, nx),
        mesh=mesh,
        in_specs=in_specs,
        out_specs=out_specs,
        check_vma=False,
    )
```
